32 devices in a mesh: seq: 4 (over z), mp: 4 (over y, x), req: 2 (over core).
Axes of the slice: x: 2, y: 2, z: 4, core: 2. Of those that a mesh axis runs over, the one named last changes fastest.
Arguments:
- hidden: bfloat16 [2, 1024, 3072], P('req', 'seq', 'mp'), may hold values from -6 to 6
- norm_gain: bfloat16 [3072], replicated, may hold values from 0.5 to 1.5
- w_query: bfloat16 [3072, 1024], P(None, 'mp'), may hold values from -0.109375 to 0.109375
- w_keyval: bfloat16 [3072, 512], P(None, 'mp'), may hold values from -0.109375 to 0.109375
- w_attn_out: bfloat16 [1024, 3072], P('mp'), may hold values from -1.5 to 1.5
- w_inner: bfloat16 [3072, 2, 1536], P(None, None, 'mp'), may hold values from -0.109375 to 0.109375
- w_bc: bfloat16 [3072, 512], P(None, 'mp'), may hold values from -0.109375 to 0.109375
- w_dt: bfloat16 [3072, 12], P(None, 'mp'), may hold values from -0.109375 to 0.109375
- dt_bias: float32 [12], P('mp'), may hold values from -4 to 0
- a_log: float32 [12], P('mp'), may hold values from -12 to 0
- d_skip: float32 [12], P('mp'), may hold values from 0.1 to 10
- conv_x: bfloat16 [4, 1536], P(None, 'mp'), may hold values from -3 to 3
- conv_bc: bfloat16 [4, 512], replicated, may hold values from -3 to 3
- mamba_gain: bfloat16 [1536], P('mp'), may hold values from 0.5 to 1.5
- w_mamba_out: bfloat16 [1536, 3072], P('mp'), may hold values from -0.15625 to 0.15625
- cache: bfloat16 [2, 1024, 512], P('req', 'seq', 'mp'), may hold values from -70 to 70, as said below
- cache_len: int32 [2], P('req'), may hold values from 256 to 1024
- tail_x: bfloat16 [2, 3, 1536], P('req', None, 'mp'), may hold values from -6 to 6
- tail_bc: bfloat16 [2, 3, 512], P('req'), may hold values from -6 to 6
- ssm_init: float32 [2, 12, 128, 256], P('req', 'mp'), may hold values from -6 to 6
Outputs:
- layer_out: bfloat16 [2, 1024, 3072], P('req', 'seq', 'mp')
- new_keyval: bfloat16 [2, 1024, 512], P('req', 'seq', 'mp')
- block_states: float32 [2, 4, 12, 128, 256], P('req', 'seq', 'mp')
The draws below stay inside these ranges and needn't reach their ends.
Inputs may be any that keep to these rules, and one draw needn't show every extreme that they name: Rows of the cache at or past cache_len are unused.
All inputs are finite; a program needn't handle non-finite values.
Results may differ from the reference program's by a relative error of at most 0.0097.
Values may be sent and summed in bfloat16 or wider, within the bound.
No kernel may reach another device: no remote copies, remote signals or barrier semaphores. Data moves between devices by JAX's collectives and lax.ppermute only.
A program may use at most 192 MiB of HBM per device.

```python
import math
import jax
import jax.numpy as jnp
import numpy as np
from jax import lax

D = 3072
HD = 128
QH = 8
KVH = 2
MH = 12
NS = 256
CONV = 4
NEW_DEV = 256
CACHE_DEV = 256
REQS = 2
SEQ_BLOCKS = 4
NEW = 1024
CACHE = 1024


def draw_cache(key, part):
    first_key = jax.random.fold_in(key, 0)
    shape = (REQS, CACHE, 2 * KVH * HD)
    column = jnp.arange(2 * KVH * HD)
    is_key = (column // HD % 2 == 0)[None, None, :]
    scales = jnp.where(is_key, 2.0, 1.0)
    base = jnp.clip(jax.random.normal(first_key, shape, jnp.float32), -4.0, 4.0) * scales
    return base.astype(jnp.bfloat16)


def block_levels(rng, dims, cuts, least, top_value):
    factor_of, own = 1.0, jax.random.fold_in(rng, 6)
    for axis_at, shards_of in cuts:
        steps = jnp.exp(jax.random.uniform(jax.random.fold_in(own, axis_at), (shards_of,), jnp.float32, least / len(cuts), top_value / len(cuts)))
        factor_of = factor_of * jnp.repeat(steps, dims[axis_at] // shards_of).reshape([-1 if axis == axis_at else 1 for axis in range(len(dims))])
    return factor_of


def gaussian(rng, extent, width, limit, cuts=(), held_as=jnp.bfloat16):
    loudness = block_levels(rng, extent, cuts, -0.22, 0.18) if cuts else 1.0
    entries = jax.random.normal(rng, extent, jnp.float32) * width * loudness
    return jnp.minimum(jnp.maximum(entries, -limit), limit).astype(held_as)


def setup_inputs(seed: int = 0) -> dict:
    splits = jax.random.split(jax.random.key(seed), 21)
    hidden = gaussian(splits[0], (REQS, NEW, D), 1.0, 6.0, ((0, 2), (1, 4), (2, 4)))
    norm_gain = jnp.clip(1.0 + 0.1 * jax.random.normal(splits[1], (D,), jnp.float32), 0.5, 1.5).astype(jnp.bfloat16)
    w_query = gaussian(splits[2], (D, QH * HD), D ** -0.5, 0.109375, ((1, 4),))
    w_keyval = gaussian(splits[3], (D, 2 * KVH * HD), D ** -0.5, 0.109375, ((1, 4),))
    w_attn_out = gaussian(splits[4], (QH * HD, D), (HD // 8) ** -0.5, 1.5, ((0, 4),))
    w_inner = gaussian(splits[5], (D, 2, MH * HD), D ** -0.5, 0.109375, ((2, 4),))
    w_bc = gaussian(splits[6], (D, 2 * NS), D ** -0.5, 0.109375, ((1, 4),))
    w_dt = gaussian(splits[7], (D, MH), D ** -0.5, 0.109375, ((1, 4),))
    dt_bias = jnp.clip(-4.0 + 4.0 * jax.random.uniform(splits[8], (MH,), jnp.float32) ** block_levels(splits[8], (MH,), ((0, 4),), -0.2, 0.2), -4.0, 0.0)
    a_log = jnp.clip(-12.0 + 12.0 * jax.random.uniform(splits[9], (MH,), jnp.float32) ** block_levels(splits[9], (MH,), ((0, 4),), -0.2, 0.2), -12.0, 0.0)
    d_skip = jnp.clip(jnp.exp(math.log(10.0) - 4.6051702 * jax.random.uniform(splits[10], (MH,), jnp.float32) ** block_levels(splits[10], (MH,), ((0, 4),), -0.2, 0.2)), 0.1, 10.0)
    conv_x = gaussian(splits[11], (CONV, MH * HD), CONV ** -0.5, 3.0, ((1, 4),))
    conv_bc = gaussian(splits[12], (CONV, 2 * NS), CONV ** -0.5, 3.0)
    mamba_gain = jnp.clip(1.0 + 0.1 * jax.random.normal(splits[13], (MH * HD,), jnp.float32), 0.5, 1.5).astype(jnp.bfloat16)
    w_mamba_out = gaussian(splits[14], (MH * HD, D), (MH * HD) ** -0.5, 0.15625, ((0, 4),))
    cache = draw_cache(jax.random.fold_in(splits[20], 71), 0)
    cache_len = jax.random.randint(splits[16], (REQS,), CACHE_DEV, CACHE + 1).astype(jnp.int32)
    tail_x = gaussian(splits[17], (REQS, CONV - 1, MH * HD), 1.0, 6.0, ((0, 2), (2, 4)))
    tail_bc = gaussian(splits[18], (REQS, CONV - 1, 2 * NS), 1.0, 6.0, ((0, 2),))
    ssm_init = gaussian(splits[19], (REQS, MH, HD, NS), 1.0, 6.0, ((0, 2), (1, 4)), jnp.float32)
    return {"hidden": hidden, "norm_gain": norm_gain, "w_query": w_query, "w_keyval": w_keyval, "w_attn_out": w_attn_out, "w_inner": w_inner, "w_bc": w_bc, "w_dt": w_dt, "dt_bias": dt_bias, "a_log": a_log, "d_skip": d_skip, "conv_x": conv_x, "conv_bc": conv_bc, "mamba_gain": mamba_gain, "w_mamba_out": w_mamba_out, "cache": cache, "cache_len": cache_len, "tail_x": tail_x, "tail_bc": tail_bc, "ssm_init": ssm_init}


epsilon = 1e-05
rope_base = 100000000000.0
negative = -1e+30

def rotate(values, positions):
    half = HD // 2
    freqs = rope_base ** (-jnp.arange(half, dtype=jnp.float32) * 2.0 / HD)
    angles = positions.astype(jnp.float32)[:, None] * freqs[None, :]
    cosine = jnp.cos(angles)[:, None, :]
    sine = jnp.sin(angles)[:, None, :]
    first = values[..., :half]
    second = values[..., half:]
    return jnp.concatenate([first * cosine - second * sine, second * cosine + first * sine], axis=-1)

def rms_scale(values):
    mean_sq = lax.optimization_barrier(jnp.mean(values * values, axis=-1, keepdims=True))
    return values * lax.rsqrt(mean_sq + epsilon)

def causal_conv(tail, inputs, taps):
    padded = jnp.concatenate([tail, inputs], axis=0).astype(jnp.float32)
    count = inputs.shape[0]
    total = jnp.zeros(inputs.shape, jnp.float32)
    for offset in range(CONV):
        total = total + taps[offset].astype(jnp.float32)[None, :] * padded[offset:offset + count]
    return jax.nn.silu(total)

def one_request(hidden_r, norm_gain, w_query, w_keyval, w_attn_out, w_inner, w_bc, w_dt, dt_bias, a_log, d_skip, conv_x, conv_bc, mamba_gain, w_mamba_out, cache_r, length, tail_xr, tail_bcr, init_r):
    high = lax.Precision.HIGHEST
    normed = (rms_scale(hidden_r.astype(jnp.float32)) * norm_gain.astype(jnp.float32)).astype(jnp.bfloat16)
    positions = length + jnp.arange(NEW, dtype=jnp.int32)
    query = rotate(jnp.dot(normed, w_query, preferred_element_type=jnp.float32).reshape(NEW, QH, HD), positions)
    query = query.astype(jnp.bfloat16)
    projected = jnp.dot(normed, w_keyval, preferred_element_type=jnp.float32).reshape(NEW, 2 * KVH, HD)
    is_key = (jnp.arange(2 * KVH) % 2 == 0)[None, :, None]
    new_kv = jnp.where(is_key, rotate(projected, positions), projected).astype(jnp.bfloat16)
    new_flat = new_kv.reshape(NEW, 2 * KVH * HD)
    bc_proj = jnp.dot(normed, w_bc, preferred_element_type=jnp.float32).astype(jnp.bfloat16)
    inner = jnp.einsum('td,dkc->tkc', normed.astype(jnp.float32), w_inner.astype(jnp.float32)).astype(jnp.bfloat16)
    gate_z = inner[:, 0]
    x_in = inner[:, 1]
    x_conv = causal_conv(tail_xr, x_in, conv_x).reshape(NEW, MH, HD)
    bc_conv = causal_conv(tail_bcr, bc_proj, conv_bc)
    b_mat = bc_conv[:, :NS]
    c_mat = bc_conv[:, NS:]
    step_size = jax.nn.softplus(jnp.dot(normed, w_dt, preferred_element_type=jnp.float32) + dt_bias.astype(jnp.float32))
    log_decay = -step_size * jnp.exp(a_log.astype(jnp.float32))[None, :]

    def token(state, inputs):
        decay_t, step_t, x_t, b_t, c_t = inputs
        state = jnp.exp(decay_t)[:, None, None] * state + (step_t[:, None] * x_t)[:, :, None] * b_t[None, None, :]
        return (state, jnp.einsum('hpn,n->hp', state, c_t, precision=high))

    def block(state, inputs):
        state, outputs = lax.scan(token, state, inputs)
        return (state, (outputs, state))
    blocked = (log_decay.reshape(SEQ_BLOCKS, NEW_DEV, MH), step_size.reshape(SEQ_BLOCKS, NEW_DEV, MH), x_conv.reshape(SEQ_BLOCKS, NEW_DEV, MH, HD), b_mat.reshape(SEQ_BLOCKS, NEW_DEV, NS), c_mat.reshape(SEQ_BLOCKS, NEW_DEV, NS))
    final_state, (outputs, states) = lax.scan(block, init_r.astype(jnp.float32), blocked)
    mamba_y = outputs.reshape(NEW, MH, HD) + d_skip.astype(jnp.float32)[None, :, None] * x_conv
    gated = mamba_y * jax.nn.silu(gate_z.astype(jnp.float32).reshape(NEW, MH, HD))
    mixed = (rms_scale(gated).reshape(NEW, MH * HD) * mamba_gain.astype(jnp.float32)).astype(jnp.bfloat16)
    cache_heads = cache_r.reshape(CACHE, 2 * KVH, HD)
    keys = jnp.concatenate([cache_heads[:, 0::2], new_kv[:, 0::2]], axis=0).astype(jnp.float32)
    values = jnp.concatenate([cache_heads[:, 1::2], new_kv[:, 1::2]], axis=0).astype(jnp.float32)
    group_of = np.arange(QH) // (QH // KVH)
    keys_head = jnp.transpose(keys, (1, 0, 2))[group_of]
    values_head = jnp.transpose(values, (1, 0, 2))[group_of]
    cache_ok = jnp.arange(CACHE, dtype=jnp.int32) < length
    scale = 1.0 / math_sqrt(HD)

    def attend(index):
        start = index * NEW_DEV
        query_block = lax.dynamic_slice_in_dim(query, start, NEW_DEV, 0).astype(jnp.float32)
        query_index = start + jnp.arange(NEW_DEV, dtype=jnp.int32)
        new_ok = jnp.arange(NEW, dtype=jnp.int32)[None, :] <= query_index[:, None]
        valid = jnp.concatenate([jnp.broadcast_to(cache_ok[None, :], (NEW_DEV, CACHE)), new_ok], axis=1)
        scores = jnp.einsum('qhd,hkd->hqk', query_block, keys_head) * scale
        masked = jnp.where(valid[None], scores, negative)
        top = lax.optimization_barrier(jnp.max(masked, axis=-1, keepdims=True))
        weights = jnp.where(valid[None], jnp.exp(masked - top), 0.0)
        rounded = lax.optimization_barrier(weights.astype(jnp.bfloat16)).astype(jnp.float32)
        summed = jnp.einsum('hqk,hkd->qhd', rounded, values_head)
        return (summed / jnp.transpose(lax.optimization_barrier(jnp.sum(weights, axis=-1)))[:, :, None]).astype(jnp.bfloat16)
    attended = lax.map(attend, jnp.arange(SEQ_BLOCKS, dtype=jnp.int32)).reshape(NEW, QH * HD)
    total = jnp.dot(attended, w_attn_out, preferred_element_type=jnp.float32)
    total = total + jnp.dot(mixed, w_mamba_out, preferred_element_type=jnp.float32)
    layer = (total + hidden_r.astype(jnp.float32)).astype(jnp.bfloat16)
    return (layer, new_flat, states)

def math_sqrt(value):
    return float(value) ** 0.5

def reference(hidden, norm_gain, w_query, w_keyval, w_attn_out, w_inner, w_bc, w_dt, dt_bias, a_log, d_skip, conv_x, conv_bc, mamba_gain, w_mamba_out, cache, cache_len, tail_x, tail_bc, ssm_init):
    layers = []
    keyvals = []
    states = []
    for request in range(REQS):
        layer, new_flat, state_list = one_request(hidden[request], norm_gain, w_query, w_keyval, w_attn_out, w_inner, w_bc, w_dt, dt_bias, a_log, d_skip, conv_x, conv_bc, mamba_gain, w_mamba_out, cache[request], cache_len[request], tail_x[request], tail_bc[request], ssm_init[request])
        layers.append(layer)
        keyvals.append(new_flat)
        states.append(state_list)
    return (jnp.stack(layers), jnp.stack(keyvals), jnp.stack(states))
```

```python
import jax
import jax.numpy as jnp
from jax import lax
from jax.sharding import PartitionSpec as P

HD = 128
QH = 8
KVH = 2
NS = 256
CONV = 4
RIM = 16


epsilon = 1e-05
rope_base = 100000000000.0
negative = -1e30


def swap(block, turn):
    return lax.ppermute(block, "mp", [(i, i ^ turn) for i in range(lax.axis_size("mp"))])


def ahead(block, distance, wrap=False):
    count = lax.axis_size("seq")
    if wrap:
        return lax.ppermute(block, "seq", [(i, (i + distance) % count) for i in range(count)])
    return lax.ppermute(block, "seq", [(i, i + distance) for i in range(count - distance)])


def ahead_and_swap(block, turn):
    rows, cols = lax.axis_size("seq"), lax.axis_size("mp")
    route = [(i * cols + j, (i + 1) * cols + (j ^ turn)) for i in range(rows - 1) for j in range(cols)]
    return lax.ppermute(block, ("seq", "mp"), route)


def rotate(values, positions):
    half = HD // 2
    freqs = rope_base ** (-jnp.arange(half, dtype=jnp.float32) * 2.0 / HD)
    angles = positions.astype(jnp.float32)[:, None] * freqs[None, :]
    cosine = jnp.cos(angles)[:, None, :]
    sine = jnp.sin(angles)[:, None, :]
    first = values[..., :half]
    second = values[..., half:]
    return jnp.concatenate(
        [first * cosine - second * sine, second * cosine + first * sine], axis=-1
    )


def rms_scale(values):
    mean_sq = jnp.mean(values * values, axis=-1, keepdims=True)
    return values * lax.rsqrt(mean_sq + epsilon)


def causal_conv(padded, count, taps):
    padded = padded.astype(jnp.float32)
    total = jnp.zeros((count, padded.shape[1]), jnp.float32)
    for offset in range(CONV):
        start = RIM - CONV + 1 + offset
        total = total + taps[offset].astype(jnp.float32)[None, :] * padded[start : start + count]
    return jax.nn.silu(total)


def shards(
    hidden,
    norm_gain,
    w_query,
    w_keyval,
    w_attn_out,
    w_inner,
    w_bc,
    w_dt,
    dt_bias,
    a_log,
    d_skip,
    conv_x,
    conv_bc,
    mamba_gain,
    w_mamba_out,
    cache,
    cache_len,
    tail_x,
    tail_bc,
    ssm_init,
):
    own_rows = hidden[0]
    tokens, width = own_rows.shape
    half_rows = tokens // 2
    seq_pos = lax.axis_index("seq")
    mp_pos = lax.axis_index("mp")
    n_seq = lax.axis_size("seq")
    n_mp = lax.axis_size("mp")
    length = cache_len[0]

    def natural(parts):
        out = jnp.zeros((parts[0].shape[0], parts[0].shape[1] * n_mp), parts[0].dtype)
        for turn, part in enumerate(parts):
            out = lax.dynamic_update_slice(out, part, (0, (mp_pos ^ turn) * part.shape[1]))
        return out

    from_x = swap(own_rows, 1)
    from_y = swap(own_rows, 2)
    rims = [ahead_and_swap(own_rows[tokens - RIM :], turn) for turn in range(n_mp)]
    diag_top = swap(from_x[:half_rows], 2)
    diag_low = swap(from_y[half_rows:], 1)
    diag = jnp.concatenate([diag_top, diag_low], axis=0)
    whole = natural(
        [jnp.concatenate([r, c], axis=0) for r, c in zip(rims, [own_rows, from_x, from_y, diag])]
    )
    normed = (rms_scale(whole.astype(jnp.float32)) * norm_gain.astype(jnp.float32)).astype(
        jnp.bfloat16
    )
    positions = length + seq_pos * tokens + jnp.arange(tokens, dtype=jnp.int32)
    local_heads = w_query.shape[1] // HD
    bc_block = jnp.dot(normed, w_bc, preferred_element_type=jnp.float32).astype(jnp.bfloat16)
    bc_parts = [bc_block] + [swap(bc_block, turn) for turn in (1, 2, 3)]
    current = normed[RIM:]
    query = rotate(
        jnp.dot(current, w_query, preferred_element_type=jnp.float32).reshape(
            tokens, local_heads, HD
        ),
        positions,
    ).astype(jnp.bfloat16)
    projected = jnp.dot(current, w_keyval, preferred_element_type=jnp.float32)
    roped = rotate(projected[:, None, :], positions)[:, 0, :]
    kv_block = jnp.where(mp_pos % 2 == 0, roped, projected).astype(jnp.bfloat16)

    owners = [(seq_pos + n_seq - step) % n_seq for step in range(n_seq)]
    if n_seq <= 4:
        cached = [cache[0]] + [ahead(cache[0], step, True) for step in range(1, n_seq)]
        fresh = [kv_block] + [ahead(kv_block, step) for step in range(1, n_seq)]
        mine = jnp.concatenate(cached + fresh, axis=0)
        starts = jnp.stack(owners)
    else:
        cached = lax.all_gather(cache[0], "seq", axis=0, tiled=True)
        fresh = lax.all_gather(kv_block, "seq", axis=0, tiled=True)
        mine = jnp.concatenate([cached, fresh], axis=0)
        starts = jnp.arange(n_seq)
    other = swap(mine, 1)
    is_key = mp_pos % 2 == 0
    keys = jnp.where(is_key, mine, other)
    values = jnp.where(is_key, other, mine)

    inner = jnp.einsum("td,dkc->ktc", normed, w_inner, preferred_element_type=jnp.float32).astype(
        jnp.bfloat16
    )
    gate_z = inner[0, RIM:]
    x_in = inner[1]
    first_block = seq_pos == 0

    def rimmed(block, tail):
        top = jnp.concatenate([jnp.zeros((RIM - CONV + 1, tail.shape[1]), tail.dtype), tail], axis=0)
        return jnp.concatenate([jnp.where(first_block, top, block[:RIM]), block[RIM:]], axis=0)

    mamba_heads = dt_bias.shape[0]
    x_conv = causal_conv(rimmed(x_in, tail_x[0]), tokens, conv_x).reshape(tokens, mamba_heads, HD)
    bc_conv = causal_conv(rimmed(natural(bc_parts), tail_bc[0]), tokens, conv_bc)
    b_mat = bc_conv[:, :NS].astype(jnp.bfloat16)
    c_mat = bc_conv[:, NS:].astype(jnp.bfloat16)
    step_size = jax.nn.softplus(
        jnp.dot(current, w_dt, preferred_element_type=jnp.float32) + dt_bias
    )
    log_decay = -step_size * jnp.exp(a_log)[None, :]
    cumulative = jnp.cumsum(log_decay, axis=0)
    block_log = cumulative[-1]
    to_end = jnp.exp(block_log[None, :] - cumulative) * step_size
    weighted = (to_end[:, :, None] * x_conv).astype(jnp.bfloat16)
    own_state = jnp.einsum("shp,sn->hpn", weighted, b_mat, preferred_element_type=jnp.float32)

    def grown(log):
        return jnp.exp(log)[:, None, None]

    prior = ahead(own_state.astype(jnp.bfloat16), 1).astype(jnp.float32)
    prior_log = ahead(block_log, 1)
    window = 1
    while window < n_seq - 1:
        with_own = (own_state + grown(block_log) * prior).astype(jnp.bfloat16)
        more = ahead(with_own, window + 1).astype(jnp.float32)
        more_log = ahead(block_log + prior_log, window + 1)
        prior = prior + grown(prior_log) * more
        prior_log = prior_log + more_log
        window = 2 * window + 1
    incoming = prior + grown(prior_log) * ssm_init[0]
    state_after = grown(block_log) * incoming + own_state

    pairs = jnp.dot(c_mat, b_mat.T, preferred_element_type=jnp.float32)
    gap = cumulative.T[:, :, None] - cumulative.T[:, None, :]
    token_ids = jnp.arange(tokens)
    lower = (token_ids[:, None] >= token_ids[None, :])[None]
    decay = jnp.exp(jnp.where(lower, gap, negative))
    mixing = (decay * pairs[None] * step_size.T[:, None, :]).astype(jnp.bfloat16)
    inner_out = jnp.einsum(
        "hts,shp->thp", mixing, x_conv.astype(jnp.bfloat16), preferred_element_type=jnp.float32
    )
    carried = jnp.exp(cumulative)[:, :, None] * jnp.einsum(
        "tn,hpn->thp", c_mat, incoming.astype(jnp.bfloat16), preferred_element_type=jnp.float32
    )
    mamba_y = inner_out + carried + d_skip[None, :, None] * x_conv
    gated = mamba_y * jax.nn.silu(gate_z.astype(jnp.float32).reshape(tokens, mamba_heads, HD))
    mixed = (
        rms_scale(gated).reshape(tokens, mamba_heads * HD) * mamba_gain.astype(jnp.float32)
    ).astype(jnp.bfloat16)

    cache_rows = cache.shape[1]
    query_index = seq_pos * tokens + jnp.arange(tokens, dtype=jnp.int32)
    slots = (starts[:, None] * cache_rows + jnp.arange(cache_rows, dtype=jnp.int32)).reshape(-1)
    news = (starts[:, None] * tokens + jnp.arange(tokens, dtype=jnp.int32)).reshape(-1)
    valid = jnp.concatenate(
        [
            jnp.broadcast_to((slots < length)[None], (tokens, slots.shape[0])),
            news[None, :] <= query_index[:, None],
        ],
        axis=1,
    )
    scale = 1.0 / float(HD) ** 0.5
    scores = jnp.einsum("qhd,kd->hqk", query, keys, preferred_element_type=jnp.float32) * scale
    masked = jnp.where(valid[None], scores, negative)
    top = jnp.max(masked, axis=-1)
    weights = jnp.where(valid[None], jnp.exp(masked - top[:, :, None]), 0.0)
    total = jnp.sum(weights, axis=-1)
    accum = jnp.einsum(
        "hqk,kd->hqd", weights.astype(jnp.bfloat16), values, preferred_element_type=jnp.float32
    )
    attended = jnp.transpose(accum / total[:, :, None], (1, 0, 2)).reshape(tokens, local_heads * HD)
    attended = attended.astype(jnp.bfloat16)

    term = jnp.dot(attended, w_attn_out, preferred_element_type=jnp.float32)
    term = term + jnp.dot(mixed, w_mamba_out, preferred_element_type=jnp.float32)
    part = [
        lax.dynamic_slice_in_dim(term, (mp_pos ^ turn) * width, width, 1) for turn in range(n_mp)
    ]
    top_part = [p[:half_rows] for p in part]
    low_part = [p[half_rows:] for p in part]

    def packed(*blocks):
        return jnp.concatenate(blocks, axis=0).astype(jnp.bfloat16)

    top_in = swap(packed(top_part[1], top_part[3]), 1).astype(jnp.float32)
    low_in = swap(packed(low_part[2], low_part[3]), 2).astype(jnp.float32)
    top_last = swap((top_part[2] + top_in[half_rows:]).astype(jnp.bfloat16), 2)
    low_last = swap((low_part[1] + low_in[half_rows:]).astype(jnp.bfloat16), 1)
    summed = jnp.concatenate(
        [
            top_part[0] + top_in[:half_rows] + top_last.astype(jnp.float32),
            low_part[0] + low_in[:half_rows] + low_last.astype(jnp.float32),
        ],
        axis=0,
    )
    layer = (summed + own_rows.astype(jnp.float32)).astype(jnp.bfloat16)
    return (layer[None], kv_block[None], state_after[None, None])


def solution(mesh):
    placed = (
        P("req", "seq", "mp"),
        P(),
        P(None, "mp"),
        P(None, "mp"),
        P("mp", None),
        P(None, None, "mp"),
        P(None, "mp"),
        P(None, "mp"),
        P("mp"),
        P("mp"),
        P("mp"),
        P(None, "mp"),
        P(),
        P("mp"),
        P("mp", None),
        P("req", "seq", "mp"),
        P("req"),
        P("req", None, "mp"),
        P("req", None, None),
        P("req", "mp", None, None),
    )
    return jax.shard_map(
        shards,
        mesh=mesh,
        in_specs=placed,
        out_specs=(P("req", "seq", "mp"), P("req", "seq", "mp"), P("req", "seq", "mp", None, None)),
        check_vma=False,
    )
```

```python
import functools

import jax
import jax.numpy as jnp
from jax import lax
from jax.experimental import pallas as pl
from jax.experimental.pallas import tpu as pltpu
from jax.sharding import PartitionSpec as P

HD = 128
QH = 8
KVH = 2
NS = 256
CONV = 4
RIM = 16
LOGS = 32


epsilon = 1e-05
rope_base = 100000000000.0
negative = -1e30
f32 = jnp.float32
bf16 = jnp.bfloat16


def call(kernel, out_shape, n_scalars, n_arrays, micros, scratch=(), limit=24 * 1024 * 1024, left=0):
    smem = pl.BlockSpec(memory_space=pltpu.SMEM)
    vmem = pl.BlockSpec(memory_space=pltpu.VMEM)
    return pl.pallas_call(
        kernel,
        out_shape=out_shape,
        in_specs=[smem] * n_scalars + [vmem] * n_arrays + [pl.BlockSpec(memory_space=pl.ANY)] * left,
        out_specs=jax.tree.map(lambda _: vmem, out_shape),
        scratch_shapes=scratch,
        compiler_params=pltpu.CompilerParams(vmem_limit_bytes=limit),
        cost_estimate=pl.CostEstimate(flops=micros * 10**9, bytes_accessed=0, transcendentals=0),
    )


def shape(*dims, dtype=bf16):
    return jax.ShapeDtypeStruct(dims, dtype)


def swap(block, turn):
    return lax.ppermute(block, "mp", [(i, i ^ turn) for i in range(lax.axis_size("mp"))])


def cross(block, turn):
    return lax.ppermute(block, "seq", [(i, i ^ turn) for i in range(lax.axis_size("seq"))])


def ahead(block):
    count = lax.axis_size("seq")
    return lax.ppermute(block, "seq", [(i, (i + 1) % count) for i in range(count)])


def dot(a, b):
    return jnp.dot(a, b, preferred_element_type=f32)


def dot_nt(a, b):
    return lax.dot_general(a, b, (((1,), (1,)), ((), ())), preferred_element_type=f32)


def dot_tn(a, b):
    return lax.dot_general(a, b, (((0,), (0,)), ((), ())), preferred_element_type=f32)


def silu(v):
    return v / (1.0 + jnp.exp(-v))


def rope(v, cos, sin):
    return v * cos + pltpu.roll(v, HD // 2, 1) * sin


def norm_kernel(
    place, own, from_x, from_y, diag_top, diag_low, rim0, rim1, rim2, rim3, gain, w_bc, w_kv, cos, sin,
    cache, later, normed, bc, kv, packed,
):
    me = place[0]
    tokens, width = own.shape
    half = tokens // 2
    full = 1.0 / (4 * width)

    def columns(turn):
        return pl.ds(pl.multiple_of((me ^ turn) * width, 128), width)

    def rows(start, count, blocks):
        square = sum(
            jnp.sum(b.astype(f32) * b.astype(f32), axis=1, keepdims=True) for b in blocks
        )
        inverse = lax.rsqrt(square * full + epsilon)
        for turn, block in enumerate(blocks):
            scaled = block.astype(f32) * inverse * gain[:, columns(turn)]
            normed[pl.ds(start, count), columns(turn)] = scaled.astype(bf16)

    rows(0, RIM, [rim0[...], rim1[...], rim2[...], rim3[...]])
    rows(RIM, half, [own[:half], from_x[:half], from_y[:half], diag_top[...]])
    rows(RIM + half, half, [own[half:], from_x[half:], from_y[half:], diag_low[...]])
    bc[...] = dot(normed[...], w_bc[...]).astype(bf16)
    projected = dot(normed[RIM:, :], w_kv[...])
    turned = rope(projected, cos[...], sin[...])
    block = jnp.where(me % 2 == 0, turned, projected).astype(bf16)
    kv[...] = block
    packed[: cache.shape[0], :] = cache[...]
    packed[cache.shape[0] :, :] = block


def softplus(v):
    return jnp.maximum(v, 0.0) + jnp.log1p(jnp.exp(-jnp.abs(v)))


def project_kernel(
    dt_bias, a_log, normed, w_query, w_inner, w_dt, cos, sin, query, x_in, gate_z, steps, cumulative
):
    tokens = cos.shape[0]
    x_in[...] = dot(normed[...], w_inner[1]).astype(bf16)
    current = normed[RIM:, :]
    raw = jnp.concatenate([dot_nt(w_dt[...], current), jnp.zeros((5, tokens), f32)], axis=0)
    head = lax.broadcasted_iota(jnp.int32, (8, tokens), 0)
    bias = jnp.zeros((8, tokens), f32)
    rate = jnp.zeros((8, tokens), f32)
    for h in range(3):
        bias = jnp.where(head == h, dt_bias[h], bias)
        rate = jnp.where(head == h, a_log[h], rate)
    step = softplus(raw + bias)
    decay = -step * jnp.exp(rate)
    before = lax.broadcasted_iota(jnp.int32, (tokens, tokens), 0)
    after = lax.broadcasted_iota(jnp.int32, (tokens, tokens), 1)
    upper = jnp.where(before <= after, 1.0, 0.0)
    steps[...] = step
    cumulative[...] = jnp.dot(
        decay, upper, preferred_element_type=f32, precision=lax.Precision.HIGHEST
    )
    gate_z[...] = dot(current, w_inner[0]).astype(bf16)
    projected = dot(current, w_query[...])
    for h in range(projected.shape[1] // HD):
        block = pl.ds(h * HD, HD)
        query[:, block] = rope(projected[:, h * HD : (h + 1) * HD], cos[...], sin[...]).astype(bf16)


def conv(scratch, tail, taps, first, tokens):
    scratch[RIM - CONV + 1 : RIM, :] = jnp.where(
        first, tail[0].astype(f32), scratch[RIM - CONV + 1 : RIM, :]
    )
    total = None
    for offset in range(CONV):
        start = RIM - CONV + 1 + offset
        term = taps[offset : offset + 1, :].astype(f32) * scratch[start : start + tokens, :]
        total = term if total is None else total + term
    return silu(total)


def logs_of(log):
    log = jnp.maximum(log, -256.0)
    high = jnp.floor(log)
    rest = (log - high) * 256.0
    middle = jnp.floor(rest)
    low = rest - middle
    return jnp.concatenate([high, middle, low, jnp.zeros_like(low)], axis=0).astype(bf16)


def log_from(rows):
    rows = rows.astype(f32)
    return rows[0:8] + (rows[8:16] + rows[16:24]) * (1.0 / 256.0)


def state_kernel(
    place, x_in, bc0, bc1, bc2, bc3, tail_x, tail_bc, conv_x, conv_bc, steps, cumulative,
    own, packet, x_conv, b_mat, c_mat, pad_x, pad_bc,
):
    me, first = place[0], place[1] == 0
    tokens = steps.shape[1]
    for turn, part in enumerate([bc0, bc1, bc2, bc3]):
        pad_bc[:, pl.ds(pl.multiple_of((me ^ turn) * HD, HD), HD)] = part[...].astype(f32)
    pad_x[...] = x_in[...].astype(f32)
    bc = conv(pad_bc, tail_bc, conv_bc, first, tokens).astype(bf16)
    b_mat[...] = bc[:, :NS]
    c_mat[...] = bc[:, NS:]
    convolved = conv(pad_x, tail_x, conv_x, first, tokens)
    x_conv[...] = convolved.astype(bf16)
    last = cumulative[:, tokens - 1 : tokens]
    to_end = jnp.transpose(jnp.exp(last - cumulative[...]) * steps[...])
    heads = convolved.shape[1] // HD
    for h in range(heads):
        weighted = convolved[:, h * HD : (h + 1) * HD] * to_end[:, h : h + 1]
        state = dot_tn(weighted.astype(bf16), bc[:, :NS])
        own[h * HD : (h + 1) * HD, :] = state
        packet[h * HD : (h + 1) * HD, :] = state.astype(bf16)
    packet[heads * HD :, :] = logs_of(jnp.broadcast_to(last, (8, NS)))


def inside_kernel(d_skip, c_mat, b_mat, steps, cumulative, x_conv, y):
    tokens = steps.shape[1]
    pairs = dot_nt(c_mat[...], b_mat[...])
    column = jnp.transpose(cumulative[...])
    row_id = lax.broadcasted_iota(jnp.int32, (tokens, tokens), 0)
    col_id = lax.broadcasted_iota(jnp.int32, (tokens, tokens), 1)
    lower = row_id >= col_id
    for h in range(x_conv.shape[1] // HD):
        gap = column[:, h : h + 1] - cumulative[h : h + 1, :]
        mixing = jnp.exp(jnp.where(lower, gap, negative)) * pairs * steps[h : h + 1, :]
        block = x_conv[:, h * HD : (h + 1) * HD]
        y[:, h * HD : (h + 1) * HD] = dot(mixing.astype(bf16), block) + d_skip[h] * block.astype(f32)


def join_kernel(place, first, second, packet, *, bit):
    swapped = (place[1] // bit) % 2 == 0 if bit else False
    size = first.shape[0] - LOGS
    first_log, second_log = log_from(first[size:, :]), log_from(second[size:, :])
    grown = jnp.exp(jnp.where(swapped, second_log, first_log))
    for h in range(size // HD):
        block = pl.ds(h * HD, HD)
        a, b = first[block, :].astype(f32), second[block, :].astype(f32)
        later, earlier = jnp.where(swapped, b, a), jnp.where(swapped, a, b)
        packet[block, :] = (later + grown[h : h + 1, :] * earlier).astype(bf16)
    packet[size:, :] = logs_of(first_log + second_log)


def finish_kernel(
    place, near, far, init, own, c_mat, cumulative, y, gate_z, gain, attended, w_attn, w_mamba,
    states, keep, keep_top, keep_low, to_x, to_y, mixed,
):
    me = place[0]
    heads = init.shape[1]
    tokens = y.shape[0]
    half = tokens // 2
    size = heads * HD
    near_on, far_on = place[1] == 1, place[2] == 1
    near_log = jnp.where(near_on, log_from(near[size:, :]), 0.0)
    far_log = jnp.where(far_on, log_from(far[size:, :]), 0.0)
    near_grown, far_grown = jnp.exp(near_log), jnp.exp(near_log + far_log)
    block_grown = jnp.exp(
        jnp.broadcast_to(cumulative[:, tokens - 1 : tokens], (8, NS))
    )
    growth = jnp.transpose(jnp.exp(cumulative[...]))
    for h in range(heads):
        block = pl.ds(h * HD, HD)
        incoming = (
            jnp.where(near_on, near[block, :].astype(f32), 0.0)
            + near_grown[h : h + 1, :] * jnp.where(far_on, far[block, :].astype(f32), 0.0)
            + far_grown[h : h + 1, :] * init[0, h]
        )
        states[0, 0, h] = block_grown[h : h + 1, :] * incoming + own[block, :]
        carried = dot_nt(c_mat[...], incoming.astype(bf16)) * growth[:, h : h + 1]
        gated = (y[:, block] + carried) * silu(gate_z[:, block].astype(f32))
        mean_sq = jnp.sum(gated * gated, axis=1, keepdims=True) * (1.0 / HD)
        mixed[:, block] = (gated * lax.rsqrt(mean_sq + epsilon) * gain[:, block]).astype(bf16)

    width = keep.shape[1]

    def term(turn, start, count):
        columns = pl.ds(pl.multiple_of((me ^ turn) * width, 128), width)
        return dot(attended[start : start + count, :], w_attn[:, columns]) + dot(
            mixed[start : start + count, :], w_mamba[:, columns]
        )

    to_x[:half, :] = term(1, 0, half).astype(bf16)
    low_one = term(1, half, half)
    keep_low[...] = low_one
    to_y[:half, :] = term(2, half, half).astype(bf16)
    keep_top[...] = term(2, 0, half)
    to_x[half:, :] = term(3, 0, half).astype(bf16)
    to_y[half:, :] = term(3, half, half).astype(bf16)
    keep[...] = term(0, 0, tokens)


def attention_kernel(place, length, query, *refs, cache_rows, scale):
    n_seq = (len(refs) - 2) // 2
    mine, other, out, scores = refs[:n_seq], refs[n_seq : 2 * n_seq], refs[-2], refs[-1]
    key_first = place[0] % 2 == 0
    seq_pos = place[1]
    tokens = query.shape[0]
    heads = query.shape[1] // HD
    rows = heads * tokens
    count = mine[0].shape[0]
    both = jnp.concatenate([query[:, h * HD : (h + 1) * HD] for h in range(heads)], axis=0)
    row = lax.broadcasted_iota(jnp.int32, (rows, count), 0) % tokens
    col = lax.broadcasted_iota(jnp.int32, (rows, count), 1)
    highest = None
    for turn in range(n_seq):
        keys = jnp.where(key_first, mine[turn][...], other[turn][...])
        owner = seq_pos ^ turn
        left = length[0] - owner * cache_rows
        last = cache_rows + jnp.where(owner < seq_pos, tokens, jnp.where(owner > seq_pos, -1, row))
        limit = jnp.where(col < cache_rows, left, last + 1)
        part = jnp.where(col < limit, dot_nt(both, keys), negative)
        scores[:, turn * count : (turn + 1) * count] = part
        for start in range(0, count, 128):
            block = part[:, start : start + 128]
            highest = block if highest is None else jnp.maximum(highest, block)
    top = jnp.max(highest, axis=1, keepdims=True)
    total = None
    accum = jnp.zeros((rows, HD), f32)
    for turn in range(n_seq):
        values = jnp.where(key_first, other[turn][...], mine[turn][...])
        weights = jnp.exp2((scores[:, turn * count : (turn + 1) * count] - top) * (scale * 1.4426950408889634))
        for start in range(0, count, 128):
            block = weights[:, start : start + 128]
            total = block if total is None else total + block
        accum = accum + dot(weights.astype(bf16), values)
    attended = accum / jnp.sum(total, axis=1, keepdims=True)
    for h in range(heads):
        out[:, h * HD : (h + 1) * HD] = attended[h * tokens : (h + 1) * tokens].astype(bf16)


def attend_plain(query, keys, values, length, starts, cache_rows, seq_pos):
    tokens = query.shape[0]
    query_index = seq_pos * tokens + jnp.arange(tokens, dtype=jnp.int32)
    slots = (starts[:, None] * cache_rows + jnp.arange(cache_rows, dtype=jnp.int32)).reshape(-1)
    news = (starts[:, None] * tokens + jnp.arange(tokens, dtype=jnp.int32)).reshape(-1)
    valid = jnp.concatenate(
        [
            jnp.broadcast_to((slots < length)[None], (tokens, slots.shape[0])),
            news[None, :] <= query_index[:, None],
        ],
        axis=1,
    )
    heads = query.reshape(tokens, -1, HD)
    scores = jnp.einsum("qhd,kd->hqk", heads, keys, preferred_element_type=f32) * HD**-0.5
    masked = jnp.where(valid[None], scores, negative)
    top = jnp.max(masked, axis=-1)
    weights = jnp.where(valid[None], jnp.exp(masked - top[:, :, None]), 0.0)
    total = jnp.sum(weights, axis=-1)
    accum = jnp.einsum("hqk,kd->hqd", weights.astype(bf16), values, preferred_element_type=f32)
    out = jnp.transpose(accum / total[:, :, None], (1, 0, 2)).reshape(tokens, -1)
    return out.astype(bf16)


def shards(
    hidden,
    norm_gain,
    w_query,
    w_keyval,
    w_attn_out,
    w_inner,
    w_bc,
    w_dt,
    dt_bias,
    a_log,
    d_skip,
    conv_x,
    conv_bc,
    mamba_gain,
    w_mamba_out,
    cache,
    cache_len,
    tail_x,
    tail_bc,
    ssm_init,
):
    own_rows = hidden[0]
    tokens, width = own_rows.shape
    half = tokens // 2
    seq_pos = lax.axis_index("seq")
    mp_pos = lax.axis_index("mp")
    n_seq = lax.axis_size("seq")
    length = cache_len[0]
    place = jnp.stack([mp_pos, seq_pos, jnp.int32(n_seq)]).astype(jnp.int32)
    inner_width = w_inner.shape[2]
    heads = inner_width // HD
    w_pair = jnp.transpose(w_inner, (1, 0, 2))

    from_x = swap(own_rows, 1)
    from_y = swap(own_rows, 2)
    rim = ahead(own_rows[tokens - RIM :])
    diag_top = swap(from_x[:half], 2)
    diag_low = swap(from_y[half:], 1)
    rims = [rim] + [swap(rim, turn) for turn in (1, 2, 3)]

    positions = length + seq_pos * tokens + jnp.arange(tokens, dtype=jnp.int32)
    freqs = rope_base ** (-jnp.arange(HD // 2, dtype=f32) * 2.0 / HD)
    angles = positions.astype(f32)[:, None] * jnp.concatenate([freqs, freqs])[None, :]
    cos = jnp.cos(angles)
    sin = jnp.where(jnp.arange(HD)[None, :] < HD // 2, -jnp.sin(angles), jnp.sin(angles))
    gain = norm_gain.astype(f32)[None, :]
    mixer_gain = mamba_gain.astype(f32)[None, :]

    cache_rows = cache.shape[1]
    normed, bc_block, kv_block, packed = call(
        norm_kernel,
        (
            shape(RIM + tokens, 4 * width),
            shape(RIM + tokens, w_bc.shape[1]),
            shape(tokens, w_keyval.shape[1]),
            shape(cache_rows + tokens, w_keyval.shape[1]),
        ),
        1,
        15,
        3,
        left=1,
    )(
        place, own_rows, from_x, from_y, diag_top, diag_low, *rims, gain, w_bc, w_keyval, cos, sin,
        cache[0], w_pair,
    )

    bc_parts = [bc_block] + [swap(bc_block, turn) for turn in (1, 2, 3)]

    query, x_in, gate_z, steps, cumulative = call(
        project_kernel,
        (
            shape(tokens, w_query.shape[1]),
            shape(RIM + tokens, inner_width),
            shape(tokens, inner_width),
            shape(8, tokens, dtype=f32),
            shape(8, tokens, dtype=f32),
        ),
        2,
        6,
        4,
    )(dt_bias, a_log, normed, w_query, w_pair, w_dt.T, cos, sin)

    if n_seq <= 4:
        mine = [packed] + [cross(packed, turn) for turn in range(1, n_seq)]
    else:
        mine = [lax.all_gather(packed, "seq", axis=0)]
    other = [swap(block, 1) for block in mine]

    own_state, packet, x_conv, b_mat, c_mat = call(
        state_kernel,
        (
            shape(heads * HD, NS, dtype=f32),
            shape(heads * HD + LOGS, NS),
            shape(tokens, inner_width),
            shape(tokens, NS),
            shape(tokens, NS),
        ),
        1,
        11,
        2,
        scratch=[
            pltpu.VMEM((RIM + tokens, inner_width), f32),
            pltpu.VMEM((RIM + tokens, 2 * NS), f32),
        ],
    )(place, x_in, *bc_parts, tail_x, tail_bc, conv_x, conv_bc, steps, cumulative)

    def join(first, second, bit):
        return call(
            functools.partial(join_kernel, bit=bit), shape(heads * HD + LOGS, NS), 1, 2, 1
        )(place, first, second)

    near = far = jnp.zeros_like(packet)
    near_on = far_on = jnp.int32(0)
    total, group = packet, 1
    while group < n_seq:
        received = cross(total, group)
        on = (seq_pos // group) % 2
        if group * 2 == n_seq:
            far, far_on = received, on
        else:
            if n_seq == 4:
                near, near_on = received, on
            else:
                earlier = jnp.where(on == 1, received, jnp.zeros_like(received))
                near, near_on = earlier if group == 1 else join(near, earlier, 0), jnp.int32(1)
            total = join(total, received, group)
        group *= 2
    taken = jnp.stack([mp_pos, near_on, far_on]).astype(jnp.int32)

    y_inside = call(inside_kernel, shape(tokens, inner_width, dtype=f32), 1, 5, 1)(
        d_skip, c_mat, b_mat, steps, cumulative, x_conv
    )

    if n_seq <= 4:
        attended = call(
            functools.partial(attention_kernel, cache_rows=cache_rows, scale=HD**-0.5),
            shape(tokens, w_query.shape[1]),
            2,
            1 + 2 * n_seq,
            6,
            scratch=[
                pltpu.VMEM((tokens * w_query.shape[1] // HD, n_seq * (cache_rows + tokens)), f32)
            ],
        )(place, cache_len, query, *mine, *other)
    else:
        is_key = mp_pos % 2 == 0
        attended = attend_plain(
            query,
            *[
                jnp.concatenate(
                    [both[:, :cache_rows].reshape(-1, HD), both[:, cache_rows:].reshape(-1, HD)], axis=0
                )
                for both in (
                    jnp.where(is_key, mine[0], other[0]),
                    jnp.where(is_key, other[0], mine[0]),
                )
            ],
            length,
            jnp.arange(n_seq),
            cache_rows,
            seq_pos,
        )

    state_after, keep, keep_top, keep_low, to_x, to_y = call(
        finish_kernel,
        (
            shape(1, 1, heads, HD, NS, dtype=f32),
            shape(tokens, width, dtype=f32),
            shape(half, width, dtype=f32),
            shape(half, width, dtype=f32),
            shape(tokens, width),
            shape(tokens, width),
        ),
        1,
        12,
        4,
        scratch=[pltpu.VMEM((tokens, inner_width), bf16)],
    )(
        taken, near, far, ssm_init, own_state, c_mat, cumulative, y_inside, gate_z, mixer_gain,
        attended, w_attn_out, w_mamba_out,
    )

    top_in = swap(to_x, 1)
    low_in = swap(to_y, 2)
    top_last = swap((keep_top + top_in[half:].astype(f32)).astype(bf16), 2)
    low_last = swap((keep_low + low_in[half:].astype(f32)).astype(bf16), 1)
    summed = keep + own_rows.astype(f32)
    summed = summed + jnp.concatenate(
        [
            top_in[:half].astype(f32) + top_last.astype(f32),
            low_in[:half].astype(f32) + low_last.astype(f32),
        ],
        axis=0,
    )
    return (summed.astype(bf16)[None], kv_block[None], state_after)


def solution(mesh):
    placed = (
        P("req", "seq", "mp"),
        P(),
        P(None, "mp"),
        P(None, "mp"),
        P("mp", None),
        P(None, None, "mp"),
        P(None, "mp"),
        P(None, "mp"),
        P("mp"),
        P("mp"),
        P("mp"),
        P(None, "mp"),
        P(),
        P("mp"),
        P("mp", None),
        P("req", "seq", "mp"),
        P("req"),
        P("req", None, "mp"),
        P("req", None, None),
        P("req", "mp", None, None),
    )
    return jax.shard_map(
        shards,
        mesh=mesh,
        in_specs=placed,
        out_specs=(P("req", "seq", "mp"), P("req", "seq", "mp"), P("req", "seq", "mp", None, None)),
        check_vma=False,
    )
```

```python
import functools

import jax
import jax.numpy as jnp
from jax import lax
from jax.experimental import pallas as pl
from jax.experimental.pallas import tpu as pltpu
from jax.sharding import PartitionSpec as P

HD = 128
QH = 8
KVH = 2
NS = 256
CONV = 4
RIM = 16
LOGS = 32


epsilon = 1e-05
rope_base = 100000000000.0
negative = -1e30
f32 = jnp.float32
bf16 = jnp.bfloat16


def call(kernel, out_shape, n_scalars, n_arrays, micros, scratch=(), limit=24 * 1024 * 1024, left=0):
    smem = pl.BlockSpec(memory_space=pltpu.SMEM)
    vmem = pl.BlockSpec(memory_space=pltpu.VMEM)
    return pl.pallas_call(
        kernel,
        out_shape=out_shape,
        in_specs=[smem] * n_scalars + [vmem] * n_arrays + [pl.BlockSpec(memory_space=pl.ANY)] * left,
        out_specs=jax.tree.map(lambda _: vmem, out_shape),
        scratch_shapes=scratch,
        compiler_params=pltpu.CompilerParams(vmem_limit_bytes=limit),
        cost_estimate=pl.CostEstimate(flops=micros * 10**9, bytes_accessed=0, transcendentals=0),
    )


def shape(*dims, dtype=bf16):
    return jax.ShapeDtypeStruct(dims, dtype)


def swap(block, turn):
    return lax.ppermute(block, "mp", [(i, i ^ turn) for i in range(lax.axis_size("mp"))])


def cross(block, turn):
    return lax.ppermute(block, "seq", [(i, i ^ turn) for i in range(lax.axis_size("seq"))])


def ahead(block):
    count = lax.axis_size("seq")
    return lax.ppermute(block, "seq", [(i, (i + 1) % count) for i in range(count)])


def dot(a, b):
    return jnp.dot(a, b, preferred_element_type=f32)


def dot_nt(a, b):
    return lax.dot_general(a, b, (((1,), (1,)), ((), ())), preferred_element_type=f32)


def dot_tn(a, b):
    return lax.dot_general(a, b, (((0,), (0,)), ((), ())), preferred_element_type=f32)


def silu(v):
    return v / (1.0 + jnp.exp(-v))


def rope(v, cos, sin):
    return v * cos + pltpu.roll(v, HD // 2, 1) * sin


def norm_kernel(
    place, own, from_x, from_y, diag_top, diag_low, rim0, rim1, rim2, rim3, gain, w_bc, w_kv, cos, sin,
    cache, later, normed, bc, kv, packed,
):
    me = place[0]
    tokens, width = own.shape
    half = tokens // 2
    full = 1.0 / (4 * width)

    def columns(turn):
        return pl.ds(pl.multiple_of((me ^ turn) * width, 128), width)

    def rows(start, count, blocks):
        square = sum(
            jnp.sum(b.astype(f32) * b.astype(f32), axis=1, keepdims=True) for b in blocks
        )
        inverse = lax.rsqrt(square * full + epsilon)
        for turn, block in enumerate(blocks):
            scaled = block.astype(f32) * inverse * gain[:, columns(turn)]
            normed[pl.ds(start, count), columns(turn)] = scaled.astype(bf16)

    rows(0, RIM, [rim0[...], rim1[...], rim2[...], rim3[...]])
    rows(RIM, half, [own[:half], from_x[:half], from_y[:half], diag_top[...]])
    rows(RIM + half, half, [own[half:], from_x[half:], from_y[half:], diag_low[...]])
    bc[...] = dot(normed[...], w_bc[...]).astype(bf16)
    projected = dot(normed[RIM:, :], w_kv[...])
    turned = rope(projected, cos[...], sin[...])
    block = jnp.where(me % 2 == 0, turned, projected).astype(bf16)
    kv[...] = block
    packed[: cache.shape[0], :] = cache[...]
    packed[cache.shape[0] :, :] = block


def softplus(v):
    return jnp.maximum(v, 0.0) + jnp.log1p(jnp.exp(-jnp.abs(v)))


def steps_kernel(dt_bias, a_log, normed, w_inner, w_dt, x_in, steps, cumulative):
    tokens = steps.shape[1]
    x_in[...] = dot(normed[...], w_inner[1]).astype(bf16)
    raw = jnp.concatenate([dot_nt(w_dt[...], normed[RIM:, :]), jnp.zeros((5, tokens), f32)], axis=0)
    head = lax.broadcasted_iota(jnp.int32, (8, tokens), 0)
    bias = jnp.zeros((8, tokens), f32)
    rate = jnp.zeros((8, tokens), f32)
    for h in range(3):
        bias = jnp.where(head == h, dt_bias[h], bias)
        rate = jnp.where(head == h, a_log[h], rate)
    step = softplus(raw + bias)
    decay = -step * jnp.exp(rate)
    before = lax.broadcasted_iota(jnp.int32, (tokens, tokens), 0)
    after = lax.broadcasted_iota(jnp.int32, (tokens, tokens), 1)
    upper = jnp.where(before <= after, 1.0, 0.0)
    steps[...] = step
    cumulative[...] = jnp.dot(
        decay, upper, preferred_element_type=f32, precision=lax.Precision.HIGHEST
    )


def query_kernel(normed, w_query, w_inner, cos, sin, *refs):
    query, gate_z = refs[-2:]
    current = normed[RIM:, :]
    gate_z[...] = dot(current, w_inner[0]).astype(bf16)
    projected = dot(current, w_query[...])
    for h in range(projected.shape[1] // HD):
        block = pl.ds(h * HD, HD)
        query[:, block] = rope(projected[:, h * HD : (h + 1) * HD], cos[...], sin[...]).astype(bf16)


def conv(scratch, tail, taps, first, tokens):
    scratch[RIM - CONV + 1 : RIM, :] = jnp.where(
        first, tail[0].astype(f32), scratch[RIM - CONV + 1 : RIM, :]
    )
    total = None
    for offset in range(CONV):
        start = RIM - CONV + 1 + offset
        term = taps[offset : offset + 1, :].astype(f32) * scratch[start : start + tokens, :]
        total = term if total is None else total + term
    return silu(total)


def logs_of(log):
    log = jnp.maximum(log, -256.0)
    high = jnp.floor(log)
    rest = (log - high) * 256.0
    middle = jnp.floor(rest)
    low = rest - middle
    return jnp.concatenate([high, middle, low, jnp.zeros_like(low)], axis=0).astype(bf16)


def log_from(rows):
    rows = rows.astype(f32)
    return rows[0:8] + (rows[8:16] + rows[16:24]) * (1.0 / 256.0)


def state_kernel(
    place, x_in, bc0, bc1, bc2, bc3, tail_x, tail_bc, conv_x, conv_bc, steps, cumulative,
    own, packet, x_conv, b_mat, c_mat, pad_x, pad_bc,
):
    me, first = place[0], place[1] == 0
    tokens = steps.shape[1]
    for turn, part in enumerate([bc0, bc1, bc2, bc3]):
        pad_bc[:, pl.ds(pl.multiple_of((me ^ turn) * HD, HD), HD)] = part[...].astype(f32)
    pad_x[...] = x_in[...].astype(f32)
    bc = conv(pad_bc, tail_bc, conv_bc, first, tokens).astype(bf16)
    b_mat[...] = bc[:, :NS]
    c_mat[...] = bc[:, NS:]
    convolved = conv(pad_x, tail_x, conv_x, first, tokens)
    x_conv[...] = convolved.astype(bf16)
    last = cumulative[:, tokens - 1 : tokens]
    to_end = jnp.transpose(jnp.exp(last - cumulative[...]) * steps[...])
    heads = convolved.shape[1] // HD
    for h in range(heads):
        weighted = convolved[:, h * HD : (h + 1) * HD] * to_end[:, h : h + 1]
        state = dot_tn(weighted.astype(bf16), bc[:, :NS])
        own[h * HD : (h + 1) * HD, :] = state
        packet[h * HD : (h + 1) * HD, :] = state.astype(bf16)
    packet[heads * HD :, :] = logs_of(jnp.broadcast_to(last, (8, NS)))


def inside_kernel(d_skip, c_mat, b_mat, steps, cumulative, x_conv, y):
    tokens = steps.shape[1]
    pairs = dot_nt(c_mat[...], b_mat[...])
    column = jnp.transpose(cumulative[...])
    row_id = lax.broadcasted_iota(jnp.int32, (tokens, tokens), 0)
    col_id = lax.broadcasted_iota(jnp.int32, (tokens, tokens), 1)
    lower = row_id >= col_id
    for h in range(x_conv.shape[1] // HD):
        gap = column[:, h : h + 1] - cumulative[h : h + 1, :]
        mixing = jnp.exp(jnp.where(lower, gap, negative)) * pairs * steps[h : h + 1, :]
        block = x_conv[:, h * HD : (h + 1) * HD]
        y[:, h * HD : (h + 1) * HD] = dot(mixing.astype(bf16), block) + d_skip[h] * block.astype(f32)


def join_kernel(place, first, second, packet, *, bit):
    swapped = (place[1] // bit) % 2 == 0 if bit else False
    size = first.shape[0] - LOGS
    first_log, second_log = log_from(first[size:, :]), log_from(second[size:, :])
    grown = jnp.exp(jnp.where(swapped, second_log, first_log))
    for h in range(size // HD):
        block = pl.ds(h * HD, HD)
        a, b = first[block, :].astype(f32), second[block, :].astype(f32)
        later, earlier = jnp.where(swapped, b, a), jnp.where(swapped, a, b)
        packet[block, :] = (later + grown[h : h + 1, :] * earlier).astype(bf16)
    packet[size:, :] = logs_of(first_log + second_log)


def term_of(me, attended, mixed, w_attn, w_mamba, width):
    def term(turn, start, count):
        columns = pl.ds(pl.multiple_of((me ^ turn) * width, 128), width)
        return dot(attended[start : start + count, :], w_attn[:, columns]) + dot(
            mixed[start : start + count, :], w_mamba[:, columns]
        )

    return term


def finish_kernel(
    place, near, far, init, own, c_mat, cumulative, y, gate_z, gain, attended, w_attn, w_mamba,
    states, mixed, far_x, far_y,
):
    me = place[0]
    heads = init.shape[1]
    tokens = y.shape[0]
    half = tokens // 2
    size = heads * HD
    near_on, far_on = place[1] == 1, place[2] == 1
    near_log = jnp.where(near_on, log_from(near[size:, :]), 0.0)
    far_log = jnp.where(far_on, log_from(far[size:, :]), 0.0)
    near_grown, far_grown = jnp.exp(near_log), jnp.exp(near_log + far_log)
    block_grown = jnp.exp(
        jnp.broadcast_to(cumulative[:, tokens - 1 : tokens], (8, NS))
    )
    growth = jnp.transpose(jnp.exp(cumulative[...]))
    for h in range(heads):
        block = pl.ds(h * HD, HD)
        incoming = (
            jnp.where(near_on, near[block, :].astype(f32), 0.0)
            + near_grown[h : h + 1, :] * jnp.where(far_on, far[block, :].astype(f32), 0.0)
            + far_grown[h : h + 1, :] * init[0, h]
        )
        states[0, 0, h] = block_grown[h : h + 1, :] * incoming + own[block, :]
        carried = dot_nt(c_mat[...], incoming.astype(bf16)) * growth[:, h : h + 1]
        gated = (y[:, block] + carried) * silu(gate_z[:, block].astype(f32))
        mean_sq = jnp.sum(gated * gated, axis=1, keepdims=True) * (1.0 / HD)
        mixed[:, block] = (gated * lax.rsqrt(mean_sq + epsilon) * gain[:, block]).astype(bf16)

    term = term_of(me, attended, mixed, w_attn, w_mamba, far_x.shape[1])
    far_x[...] = term(3, 0, half).astype(bf16)
    far_y[...] = term(3, half, half).astype(bf16)


def rest_kernel(
    place, attended, mixed, w_attn, w_mamba, own, to_x, to_y, keep, keep_top, keep_low
):
    tokens, width = own.shape
    half = tokens // 2
    term = term_of(place[0], attended, mixed, w_attn, w_mamba, width)
    to_x[...] = term(1, 0, half).astype(bf16)
    to_y[...] = term(2, half, half).astype(bf16)
    keep_top[...] = term(2, 0, half)
    keep_low[...] = term(1, half, half)
    keep[...] = term(0, 0, tokens) + own[...].astype(f32)


def attention_kernel(place, length, query, *refs, cache_rows, scale):
    n_seq = (len(refs) - 2) // 2
    mine, other, out, scores = refs[:n_seq], refs[n_seq : 2 * n_seq], refs[-2], refs[-1]
    key_first = place[0] % 2 == 0
    seq_pos = place[1]
    tokens = query.shape[0]
    heads = query.shape[1] // HD
    rows = heads * tokens
    count = mine[0].shape[0]
    both = jnp.concatenate([query[:, h * HD : (h + 1) * HD] for h in range(heads)], axis=0)
    row = lax.broadcasted_iota(jnp.int32, (rows, count), 0) % tokens
    col = lax.broadcasted_iota(jnp.int32, (rows, count), 1)
    highest = None
    for turn in range(n_seq):
        keys = jnp.where(key_first, mine[turn][...], other[turn][...])
        owner = seq_pos ^ turn
        left = length[0] - owner * cache_rows
        last = cache_rows + jnp.where(owner < seq_pos, tokens, jnp.where(owner > seq_pos, -1, row))
        limit = jnp.where(col < cache_rows, left, last + 1)
        part = jnp.where(col < limit, dot_nt(both, keys), negative)
        scores[:, turn * count : (turn + 1) * count] = part
        for start in range(0, count, 128):
            block = part[:, start : start + 128]
            highest = block if highest is None else jnp.maximum(highest, block)
    top = jnp.max(highest, axis=1, keepdims=True)
    total = None
    accum = jnp.zeros((rows, HD), f32)
    for turn in range(n_seq):
        values = jnp.where(key_first, other[turn][...], mine[turn][...])
        weights = jnp.exp2((scores[:, turn * count : (turn + 1) * count] - top) * (scale * 1.4426950408889634))
        for start in range(0, count, 128):
            block = weights[:, start : start + 128]
            total = block if total is None else total + block
        accum = accum + dot(weights.astype(bf16), values)
    attended = accum / jnp.sum(total, axis=1, keepdims=True)
    for h in range(heads):
        out[:, h * HD : (h + 1) * HD] = attended[h * tokens : (h + 1) * tokens].astype(bf16)


def attend_plain(query, keys, values, length, starts, cache_rows, seq_pos):
    tokens = query.shape[0]
    query_index = seq_pos * tokens + jnp.arange(tokens, dtype=jnp.int32)
    slots = (starts[:, None] * cache_rows + jnp.arange(cache_rows, dtype=jnp.int32)).reshape(-1)
    news = (starts[:, None] * tokens + jnp.arange(tokens, dtype=jnp.int32)).reshape(-1)
    valid = jnp.concatenate(
        [
            jnp.broadcast_to((slots < length)[None], (tokens, slots.shape[0])),
            news[None, :] <= query_index[:, None],
        ],
        axis=1,
    )
    heads = query.reshape(tokens, -1, HD)
    scores = jnp.einsum("qhd,kd->hqk", heads, keys, preferred_element_type=f32) * HD**-0.5
    masked = jnp.where(valid[None], scores, negative)
    top = jnp.max(masked, axis=-1)
    weights = jnp.where(valid[None], jnp.exp(masked - top[:, :, None]), 0.0)
    total = jnp.sum(weights, axis=-1)
    accum = jnp.einsum("hqk,kd->hqd", weights.astype(bf16), values, preferred_element_type=f32)
    out = jnp.transpose(accum / total[:, :, None], (1, 0, 2)).reshape(tokens, -1)
    return out.astype(bf16)


def shards(
    hidden,
    norm_gain,
    w_query,
    w_keyval,
    w_attn_out,
    w_inner,
    w_bc,
    w_dt,
    dt_bias,
    a_log,
    d_skip,
    conv_x,
    conv_bc,
    mamba_gain,
    w_mamba_out,
    cache,
    cache_len,
    tail_x,
    tail_bc,
    ssm_init,
):
    own_rows = hidden[0]
    tokens, width = own_rows.shape
    half = tokens // 2
    seq_pos = lax.axis_index("seq")
    mp_pos = lax.axis_index("mp")
    n_seq = lax.axis_size("seq")
    length = cache_len[0]
    place = jnp.stack([mp_pos, seq_pos, jnp.int32(n_seq)]).astype(jnp.int32)
    inner_width = w_inner.shape[2]
    heads = inner_width // HD
    w_pair = jnp.transpose(w_inner, (1, 0, 2))

    from_x = swap(own_rows, 1)
    from_y = swap(own_rows, 2)
    rim = ahead(own_rows[tokens - RIM :])
    diag_top = swap(from_x[:half], 2)
    diag_low = swap(from_y[half:], 1)
    rims = [rim] + [swap(rim, turn) for turn in (1, 2, 3)]

    positions = length + seq_pos * tokens + jnp.arange(tokens, dtype=jnp.int32)
    freqs = rope_base ** (-jnp.arange(HD // 2, dtype=f32) * 2.0 / HD)
    angles = positions.astype(f32)[:, None] * jnp.concatenate([freqs, freqs])[None, :]
    cos = jnp.cos(angles)
    sin = jnp.where(jnp.arange(HD)[None, :] < HD // 2, -jnp.sin(angles), jnp.sin(angles))
    gain = norm_gain.astype(f32)[None, :]
    mixer_gain = mamba_gain.astype(f32)[None, :]

    cache_rows = cache.shape[1]
    normed, bc_block, kv_block, packed = call(
        norm_kernel,
        (
            shape(RIM + tokens, 4 * width),
            shape(RIM + tokens, w_bc.shape[1]),
            shape(tokens, w_keyval.shape[1]),
            shape(cache_rows + tokens, w_keyval.shape[1]),
        ),
        1,
        15,
        3,
        left=1,
    )(
        place, own_rows, from_x, from_y, diag_top, diag_low, *rims, gain, w_bc, w_keyval, cos, sin,
        cache[0], w_pair,
    )

    bc_parts = [bc_block] + [swap(bc_block, turn) for turn in (1, 2, 3)]

    x_in, steps, cumulative = call(
        steps_kernel,
        (
            shape(RIM + tokens, inner_width),
            shape(8, tokens, dtype=f32),
            shape(8, tokens, dtype=f32),
        ),
        2,
        3,
        2,
    )(dt_bias, a_log, normed, w_pair, w_dt.T)

    if n_seq <= 4:
        mine = [packed] + [cross(packed, turn) for turn in range(1, n_seq)]
    else:
        mine = [lax.all_gather(packed, "seq", axis=0)]
    other = [swap(block, 1) for block in mine]

    own_state, packet, x_conv, b_mat, c_mat = call(
        state_kernel,
        (
            shape(heads * HD, NS, dtype=f32),
            shape(heads * HD + LOGS, NS),
            shape(tokens, inner_width),
            shape(tokens, NS),
            shape(tokens, NS),
        ),
        1,
        11,
        2,
        scratch=[
            pltpu.VMEM((RIM + tokens, inner_width), f32),
            pltpu.VMEM((RIM + tokens, 2 * NS), f32),
        ],
    )(place, x_in, *bc_parts, tail_x, tail_bc, conv_x, conv_bc, steps, cumulative)

    def join(first, second, bit):
        return call(
            functools.partial(join_kernel, bit=bit), shape(heads * HD + LOGS, NS), 1, 2, 1
        )(place, first, second)

    near = far = jnp.zeros_like(packet)
    near_on = far_on = jnp.int32(0)
    total, group = packet, 1
    while group < n_seq:
        received = cross(total, group)
        on = (seq_pos // group) % 2
        if group * 2 == n_seq:
            far, far_on = received, on
        else:
            if n_seq == 4:
                near, near_on = received, on
            else:
                earlier = jnp.where(on == 1, received, jnp.zeros_like(received))
                near, near_on = earlier if group == 1 else join(near, earlier, 0), jnp.int32(1)
            total = join(total, received, group)
        group *= 2
    taken = jnp.stack([mp_pos, near_on, far_on]).astype(jnp.int32)

    query, gate_z = call(
        query_kernel,
        (shape(tokens, w_query.shape[1]), shape(tokens, inner_width)),
        0,
        5,
        2,
        left=1,
    )(normed, w_query, w_pair, cos, sin, b_mat)
    y_inside = call(inside_kernel, shape(tokens, inner_width, dtype=f32), 1, 5, 1)(
        d_skip, c_mat, b_mat, steps, cumulative, x_conv
    )

    if n_seq <= 4:
        attended = call(
            functools.partial(attention_kernel, cache_rows=cache_rows, scale=HD**-0.5),
            shape(tokens, w_query.shape[1]),
            2,
            1 + 2 * n_seq,
            6,
            scratch=[
                pltpu.VMEM((tokens * w_query.shape[1] // HD, n_seq * (cache_rows + tokens)), f32)
            ],
        )(place, cache_len, query, *mine, *other)
    else:
        is_key = mp_pos % 2 == 0
        attended = attend_plain(
            query,
            *[
                jnp.concatenate(
                    [both[:, :cache_rows].reshape(-1, HD), both[:, cache_rows:].reshape(-1, HD)], axis=0
                )
                for both in (
                    jnp.where(is_key, mine[0], other[0]),
                    jnp.where(is_key, other[0], mine[0]),
                )
            ],
            length,
            jnp.arange(n_seq),
            cache_rows,
            seq_pos,
        )

    state_after, mixed, far_x, far_y = call(
        finish_kernel,
        (
            shape(1, 1, heads, HD, NS, dtype=f32),
            shape(tokens, inner_width),
            shape(half, width),
            shape(half, width),
        ),
        1,
        12,
        3,
    )(
        taken, near, far, ssm_init, own_state, c_mat, cumulative, y_inside, gate_z, mixer_gain,
        attended, w_attn_out, w_mamba_out,
    )

    far_x_in = swap(far_x, 1)
    far_y_in = swap(far_y, 2)
    to_x, to_y, keep, keep_top, keep_low = call(
        rest_kernel,
        (
            shape(half, width),
            shape(half, width),
            shape(tokens, width, dtype=f32),
            shape(half, width, dtype=f32),
            shape(half, width, dtype=f32),
        ),
        1,
        5,
        2,
    )(place, attended, mixed, w_attn_out, w_mamba_out, own_rows)
    top_in = swap(to_x, 1)
    low_in = swap(to_y, 2)
    top_last = swap((keep_top + far_x_in.astype(f32)).astype(bf16), 2)
    low_last = swap((keep_low + far_y_in.astype(f32)).astype(bf16), 1)
    summed = keep + jnp.concatenate(
        [
            top_in.astype(f32) + top_last.astype(f32),
            low_in.astype(f32) + low_last.astype(f32),
        ],
        axis=0,
    )
    return (summed.astype(bf16)[None], kv_block[None], state_after)


def solution(mesh):
    placed = (
        P("req", "seq", "mp"),
        P(),
        P(None, "mp"),
        P(None, "mp"),
        P("mp", None),
        P(None, None, "mp"),
        P(None, "mp"),
        P(None, "mp"),
        P("mp"),
        P("mp"),
        P("mp"),
        P(None, "mp"),
        P(),
        P("mp"),
        P("mp", None),
        P("req", "seq", "mp"),
        P("req"),
        P("req", None, "mp"),
        P("req", None, None),
        P("req", "mp", None, None),
    )
    return jax.shard_map(
        shards,
        mesh=mesh,
        in_specs=placed,
        out_specs=(P("req", "seq", "mp"), P("req", "seq", "mp"), P("req", "seq", "mp", None, None)),
        check_vma=False,
    )
```

```python
import functools

import jax
import jax.numpy as jnp
from jax import lax
from jax.experimental import pallas as pl
from jax.experimental.pallas import tpu as pltpu
from jax.sharding import PartitionSpec as P

HD = 128
QH = 8
KVH = 2
NS = 256
CONV = 4
RIM = 16
LOGS = 32


epsilon = 1e-05
rope_base = 100000000000.0
negative = -1e30
f32 = jnp.float32
bf16 = jnp.bfloat16


def call(kernel, out_shape, n_scalars, n_arrays, micros, scratch=(), limit=24 * 1024 * 1024, left=0):
    smem = pl.BlockSpec(memory_space=pltpu.SMEM)
    vmem = pl.BlockSpec(memory_space=pltpu.VMEM)
    return pl.pallas_call(
        kernel,
        out_shape=out_shape,
        in_specs=[smem] * n_scalars + [vmem] * n_arrays + [pl.BlockSpec(memory_space=pl.ANY)] * left,
        out_specs=jax.tree.map(lambda _: vmem, out_shape),
        scratch_shapes=scratch,
        compiler_params=pltpu.CompilerParams(vmem_limit_bytes=limit),
        cost_estimate=pl.CostEstimate(flops=micros * 10**9, bytes_accessed=0, transcendentals=0),
    )


def shape(*dims, dtype=bf16):
    return jax.ShapeDtypeStruct(dims, dtype)


def swap(block, turn):
    return lax.ppermute(block, "mp", [(i, i ^ turn) for i in range(lax.axis_size("mp"))])


def cross(block, turn):
    return lax.ppermute(block, "seq", [(i, i ^ turn) for i in range(lax.axis_size("seq"))])


def ahead(block):
    count = lax.axis_size("seq")
    return lax.ppermute(block, "seq", [(i, (i + 1) % count) for i in range(count)])


def dot(a, b):
    return jnp.dot(a, b, preferred_element_type=f32)


def dot_nt(a, b):
    return lax.dot_general(a, b, (((1,), (1,)), ((), ())), preferred_element_type=f32)


def dot_tn(a, b):
    return lax.dot_general(a, b, (((0,), (0,)), ((), ())), preferred_element_type=f32)


def silu(v):
    return v / (1.0 + jnp.exp(-v))


def rope(v, cos, sin):
    return v * cos + pltpu.roll(v, HD // 2, 1) * sin


def pack_kernel(from_x, from_y, rim, *refs):
    to_y, to_x = refs[-2:]
    half = to_y.shape[0] - RIM
    to_y[:half, :] = from_x[:half]
    to_y[half:, :] = rim[...]
    to_x[:half, :] = from_y[half:]
    to_x[half:, :] = rim[...]


def norm_kernel(
    place, own, from_x, from_y, by_y, by_x, rim, diag_rim, gain, w_bc, w_kv, cos, sin,
    cache, later, normed, bc, kv, packed,
):
    me = place[0]
    tokens, width = own.shape
    half = tokens // 2
    full = 1.0 / (4 * width)

    def columns(turn):
        return pl.ds(pl.multiple_of((me ^ turn) * width, 128), width)

    def rows(start, count, blocks):
        square = sum(
            jnp.sum(b.astype(f32) * b.astype(f32), axis=1, keepdims=True) for b in blocks
        )
        inverse = lax.rsqrt(square * full + epsilon)
        for turn, block in enumerate(blocks):
            scaled = block.astype(f32) * inverse * gain[:, columns(turn)]
            normed[pl.ds(start, count), columns(turn)] = scaled.astype(bf16)

    rows(0, RIM, [rim[...], by_x[half:], by_y[half:], diag_rim[...]])
    rows(RIM, half, [own[:half], from_x[:half], from_y[:half], by_y[:half]])
    rows(RIM + half, half, [own[half:], from_x[half:], from_y[half:], by_x[:half]])
    bc[...] = dot(normed[...], w_bc[...]).astype(bf16)
    projected = dot(normed[RIM:, :], w_kv[...])
    turned = rope(projected, cos[...], sin[...])
    block = jnp.where(me % 2 == 0, turned, projected).astype(bf16)
    kv[...] = block
    packed[: cache.shape[0], :] = cache[...]
    packed[cache.shape[0] :, :] = block


def softplus(v):
    return jnp.maximum(v, 0.0) + jnp.log1p(jnp.exp(-jnp.abs(v)))


def steps_kernel(dt_bias, a_log, normed, w_inner, w_dt, x_in, steps, cumulative):
    tokens = steps.shape[1]
    x_in[...] = dot(normed[...], w_inner[1]).astype(bf16)
    raw = jnp.concatenate([dot_nt(w_dt[...], normed[RIM:, :]), jnp.zeros((5, tokens), f32)], axis=0)
    head = lax.broadcasted_iota(jnp.int32, (8, tokens), 0)
    bias = jnp.zeros((8, tokens), f32)
    rate = jnp.zeros((8, tokens), f32)
    for h in range(3):
        bias = jnp.where(head == h, dt_bias[h], bias)
        rate = jnp.where(head == h, a_log[h], rate)
    step = softplus(raw + bias)
    decay = -step * jnp.exp(rate)
    before = lax.broadcasted_iota(jnp.int32, (tokens, tokens), 0)
    after = lax.broadcasted_iota(jnp.int32, (tokens, tokens), 1)
    upper = jnp.where(before <= after, 1.0, 0.0)
    steps[...] = step
    cumulative[...] = jnp.dot(
        decay, upper, preferred_element_type=f32, precision=lax.Precision.HIGHEST
    )


def query_kernel(normed, w_query, w_inner, cos, sin, *refs):
    query, gate_z = refs[-2:]
    current = normed[RIM:, :]
    gate_z[...] = dot(current, w_inner[0]).astype(bf16)
    projected = dot(current, w_query[...])
    for h in range(projected.shape[1] // HD):
        block = pl.ds(h * HD, HD)
        query[:, block] = rope(projected[:, h * HD : (h + 1) * HD], cos[...], sin[...]).astype(bf16)


def conv(scratch, tail, taps, first, tokens):
    scratch[RIM - CONV + 1 : RIM, :] = jnp.where(
        first, tail[0].astype(f32), scratch[RIM - CONV + 1 : RIM, :]
    )
    total = None
    for offset in range(CONV):
        start = RIM - CONV + 1 + offset
        term = taps[offset : offset + 1, :].astype(f32) * scratch[start : start + tokens, :]
        total = term if total is None else total + term
    return silu(total)


def logs_of(log):
    log = jnp.maximum(log, -256.0)
    high = jnp.floor(log)
    rest = (log - high) * 256.0
    middle = jnp.floor(rest)
    low = rest - middle
    return jnp.concatenate([high, middle, low, jnp.zeros_like(low)], axis=0).astype(bf16)


def log_from(rows):
    rows = rows.astype(f32)
    return rows[0:8] + (rows[8:16] + rows[16:24]) * (1.0 / 256.0)


def state_kernel(
    place, x_in, bc0, bc1, bc2, bc3, tail_x, tail_bc, conv_x, conv_bc, steps, cumulative,
    own, packet, x_conv, b_mat, c_mat, pad_x, pad_bc,
):
    me, first = place[0], place[1] == 0
    tokens = steps.shape[1]
    for turn, part in enumerate([bc0, bc1, bc2, bc3]):
        pad_bc[:, pl.ds(pl.multiple_of((me ^ turn) * HD, HD), HD)] = part[...].astype(f32)
    pad_x[...] = x_in[...].astype(f32)
    bc = conv(pad_bc, tail_bc, conv_bc, first, tokens).astype(bf16)
    b_mat[...] = bc[:, :NS]
    c_mat[...] = bc[:, NS:]
    convolved = conv(pad_x, tail_x, conv_x, first, tokens)
    x_conv[...] = convolved.astype(bf16)
    last = cumulative[:, tokens - 1 : tokens]
    to_end = jnp.transpose(jnp.exp(last - cumulative[...]) * steps[...])
    heads = convolved.shape[1] // HD
    for h in range(heads):
        weighted = convolved[:, h * HD : (h + 1) * HD] * to_end[:, h : h + 1]
        state = dot_tn(weighted.astype(bf16), bc[:, :NS])
        own[h * HD : (h + 1) * HD, :] = state
        packet[h * HD : (h + 1) * HD, :] = state.astype(bf16)
    packet[heads * HD :, :] = logs_of(jnp.broadcast_to(last, (8, NS)))


def inside_kernel(d_skip, c_mat, b_mat, steps, cumulative, x_conv, y):
    tokens = steps.shape[1]
    pairs = dot_nt(c_mat[...], b_mat[...])
    column = jnp.transpose(cumulative[...])
    row_id = lax.broadcasted_iota(jnp.int32, (tokens, tokens), 0)
    col_id = lax.broadcasted_iota(jnp.int32, (tokens, tokens), 1)
    lower = row_id >= col_id
    for h in range(x_conv.shape[1] // HD):
        gap = column[:, h : h + 1] - cumulative[h : h + 1, :]
        mixing = jnp.exp(jnp.where(lower, gap, negative)) * pairs * steps[h : h + 1, :]
        block = x_conv[:, h * HD : (h + 1) * HD]
        y[:, h * HD : (h + 1) * HD] = dot(mixing.astype(bf16), block) + d_skip[h] * block.astype(f32)


def join_kernel(place, first, second, packet, *, bit):
    swapped = (place[1] // bit) % 2 == 0 if bit else False
    size = first.shape[0] - LOGS
    first_log, second_log = log_from(first[size:, :]), log_from(second[size:, :])
    grown = jnp.exp(jnp.where(swapped, second_log, first_log))
    for h in range(size // HD):
        block = pl.ds(h * HD, HD)
        a, b = first[block, :].astype(f32), second[block, :].astype(f32)
        later, earlier = jnp.where(swapped, b, a), jnp.where(swapped, a, b)
        packet[block, :] = (later + grown[h : h + 1, :] * earlier).astype(bf16)
    packet[size:, :] = logs_of(first_log + second_log)


def term_of(me, attended, mixed, w_attn, w_mamba, width):
    def term(turn, start, count):
        columns = pl.ds(pl.multiple_of((me ^ turn) * width, 128), width)
        return dot(attended[start : start + count, :], w_attn[:, columns]) + dot(
            mixed[start : start + count, :], w_mamba[:, columns]
        )

    return term


def finish_kernel(
    place, near, far, init, own, c_mat, cumulative, y, gate_z, gain, attended, w_attn, w_mamba,
    states, mixed, far_x, far_y,
):
    me = place[0]
    heads = init.shape[1]
    tokens = y.shape[0]
    half = tokens // 2
    size = heads * HD
    near_on, far_on = place[1] == 1, place[2] == 1
    near_log = jnp.where(near_on, log_from(near[size:, :]), 0.0)
    far_log = jnp.where(far_on, log_from(far[size:, :]), 0.0)
    near_grown, far_grown = jnp.exp(near_log), jnp.exp(near_log + far_log)
    block_grown = jnp.exp(
        jnp.broadcast_to(cumulative[:, tokens - 1 : tokens], (8, NS))
    )
    growth = jnp.transpose(jnp.exp(cumulative[...]))
    for h in range(heads):
        block = pl.ds(h * HD, HD)
        incoming = (
            jnp.where(near_on, near[block, :].astype(f32), 0.0)
            + near_grown[h : h + 1, :] * jnp.where(far_on, far[block, :].astype(f32), 0.0)
            + far_grown[h : h + 1, :] * init[0, h]
        )
        states[0, 0, h] = block_grown[h : h + 1, :] * incoming + own[block, :]
        carried = dot_nt(c_mat[...], incoming.astype(bf16)) * growth[:, h : h + 1]
        gated = (y[:, block] + carried) * silu(gate_z[:, block].astype(f32))
        mean_sq = jnp.sum(gated * gated, axis=1, keepdims=True) * (1.0 / HD)
        mixed[:, block] = (gated * lax.rsqrt(mean_sq + epsilon) * gain[:, block]).astype(bf16)

    term = term_of(me, attended, mixed, w_attn, w_mamba, far_x.shape[1])
    far_x[...] = term(3, 0, half).astype(bf16)
    far_y[...] = term(3, half, half).astype(bf16)


def near_kernel(place, attended, mixed, w_attn, w_mamba, to_x, to_y):
    half, width = to_x.shape
    term = term_of(place[0], attended, mixed, w_attn, w_mamba, width)
    to_x[...] = term(1, 0, half).astype(bf16)
    to_y[...] = term(2, half, half).astype(bf16)


def keep_kernel(place, attended, mixed, w_attn, w_mamba, own, sent, keep, keep_top, keep_low):
    tokens, width = own.shape
    half = tokens // 2
    term = term_of(place[0], attended, mixed, w_attn, w_mamba, width)
    keep_top[...] = term(2, 0, half)
    keep_low[...] = term(1, half, half)
    keep[...] = term(0, 0, tokens) + own[...].astype(f32)


def attention_kernel(place, length, query, *refs, cache_rows, scale):
    n_seq = (len(refs) - 2) // 2
    mine, other, out, scores = refs[:n_seq], refs[n_seq : 2 * n_seq], refs[-2], refs[-1]
    key_first = place[0] % 2 == 0
    seq_pos = place[1]
    tokens = query.shape[0]
    heads = query.shape[1] // HD
    rows = heads * tokens
    count = mine[0].shape[0]
    both = jnp.concatenate([query[:, h * HD : (h + 1) * HD] for h in range(heads)], axis=0)
    row = lax.broadcasted_iota(jnp.int32, (rows, count), 0) % tokens
    col = lax.broadcasted_iota(jnp.int32, (rows, count), 1)
    highest = None
    for turn in range(n_seq):
        keys = jnp.where(key_first, mine[turn][...], other[turn][...])
        owner = seq_pos ^ turn
        left = length[0] - owner * cache_rows
        last = cache_rows + jnp.where(owner < seq_pos, tokens, jnp.where(owner > seq_pos, -1, row))
        limit = jnp.where(col < cache_rows, left, last + 1)
        part = jnp.where(col < limit, dot_nt(both, keys), negative)
        scores[:, turn * count : (turn + 1) * count] = part
        for start in range(0, count, 128):
            block = part[:, start : start + 128]
            highest = block if highest is None else jnp.maximum(highest, block)
    top = jnp.max(highest, axis=1, keepdims=True)
    total = None
    accum = jnp.zeros((rows, HD), f32)
    for turn in range(n_seq):
        values = jnp.where(key_first, other[turn][...], mine[turn][...])
        weights = jnp.exp2((scores[:, turn * count : (turn + 1) * count] - top) * (scale * 1.4426950408889634))
        for start in range(0, count, 128):
            block = weights[:, start : start + 128]
            total = block if total is None else total + block
        accum = accum + dot(weights.astype(bf16), values)
    attended = accum / jnp.sum(total, axis=1, keepdims=True)
    for h in range(heads):
        out[:, h * HD : (h + 1) * HD] = attended[h * tokens : (h + 1) * tokens].astype(bf16)


def attend_plain(query, keys, values, length, starts, cache_rows, seq_pos):
    tokens = query.shape[0]
    query_index = seq_pos * tokens + jnp.arange(tokens, dtype=jnp.int32)
    slots = (starts[:, None] * cache_rows + jnp.arange(cache_rows, dtype=jnp.int32)).reshape(-1)
    news = (starts[:, None] * tokens + jnp.arange(tokens, dtype=jnp.int32)).reshape(-1)
    valid = jnp.concatenate(
        [
            jnp.broadcast_to((slots < length)[None], (tokens, slots.shape[0])),
            news[None, :] <= query_index[:, None],
        ],
        axis=1,
    )
    heads = query.reshape(tokens, -1, HD)
    scores = jnp.einsum("qhd,kd->hqk", heads, keys, preferred_element_type=f32) * HD**-0.5
    masked = jnp.where(valid[None], scores, negative)
    top = jnp.max(masked, axis=-1)
    weights = jnp.where(valid[None], jnp.exp(masked - top[:, :, None]), 0.0)
    total = jnp.sum(weights, axis=-1)
    accum = jnp.einsum("hqk,kd->hqd", weights.astype(bf16), values, preferred_element_type=f32)
    out = jnp.transpose(accum / total[:, :, None], (1, 0, 2)).reshape(tokens, -1)
    return out.astype(bf16)


def shards(
    hidden,
    norm_gain,
    w_query,
    w_keyval,
    w_attn_out,
    w_inner,
    w_bc,
    w_dt,
    dt_bias,
    a_log,
    d_skip,
    conv_x,
    conv_bc,
    mamba_gain,
    w_mamba_out,
    cache,
    cache_len,
    tail_x,
    tail_bc,
    ssm_init,
):
    own_rows = hidden[0]
    tokens, width = own_rows.shape
    half = tokens // 2
    seq_pos = lax.axis_index("seq")
    mp_pos = lax.axis_index("mp")
    n_seq = lax.axis_size("seq")
    length = cache_len[0]
    place = jnp.stack([mp_pos, seq_pos, jnp.int32(n_seq)]).astype(jnp.int32)
    inner_width = w_inner.shape[2]
    heads = inner_width // HD
    w_pair = jnp.transpose(w_inner, (1, 0, 2))

    from_x = swap(own_rows, 1)
    from_y = swap(own_rows, 2)
    rim = ahead(own_rows[tokens - RIM :])
    positions = length + seq_pos * tokens + jnp.arange(tokens, dtype=jnp.int32)
    freqs = rope_base ** (-jnp.arange(HD // 2, dtype=f32) * 2.0 / HD)
    angles = positions.astype(f32)[:, None] * jnp.concatenate([freqs, freqs])[None, :]
    cos = jnp.cos(angles)
    sin = jnp.where(jnp.arange(HD)[None, :] < HD // 2, -jnp.sin(angles), jnp.sin(angles))
    gain = norm_gain.astype(f32)[None, :]
    mixer_gain = mamba_gain.astype(f32)[None, :]

    to_y, to_x = call(
        pack_kernel, (shape(half + RIM, width), shape(half + RIM, width)), 0, 3, 3
    )(from_x, from_y, rim)
    by_y = swap(to_y, 2)
    by_x = swap(to_x, 1)
    diag_rim = swap(rim, 3)

    cache_rows = cache.shape[1]
    normed, bc_block, kv_block, packed = call(
        norm_kernel,
        (
            shape(RIM + tokens, 4 * width),
            shape(RIM + tokens, w_bc.shape[1]),
            shape(tokens, w_keyval.shape[1]),
            shape(cache_rows + tokens, w_keyval.shape[1]),
        ),
        1,
        13,
        3,
        left=1,
    )(
        place, own_rows, from_x, from_y, by_y, by_x, rim, diag_rim, gain, w_bc, w_keyval, cos, sin,
        cache[0], w_pair,
    )

    bc_parts = [bc_block] + [swap(bc_block, turn) for turn in (1, 2, 3)]

    x_in, steps, cumulative = call(
        steps_kernel,
        (
            shape(RIM + tokens, inner_width),
            shape(8, tokens, dtype=f32),
            shape(8, tokens, dtype=f32),
        ),
        2,
        3,
        2,
    )(dt_bias, a_log, normed, w_pair, w_dt.T)

    if n_seq <= 4:
        mine = [packed] + [cross(packed, turn) for turn in range(1, n_seq)]
    else:
        mine = [lax.all_gather(packed, "seq", axis=0)]
    other = [swap(block, 1) for block in mine]

    own_state, packet, x_conv, b_mat, c_mat = call(
        state_kernel,
        (
            shape(heads * HD, NS, dtype=f32),
            shape(heads * HD + LOGS, NS),
            shape(tokens, inner_width),
            shape(tokens, NS),
            shape(tokens, NS),
        ),
        1,
        11,
        2,
        scratch=[
            pltpu.VMEM((RIM + tokens, inner_width), f32),
            pltpu.VMEM((RIM + tokens, 2 * NS), f32),
        ],
    )(place, x_in, *bc_parts, tail_x, tail_bc, conv_x, conv_bc, steps, cumulative)

    def join(first, second, bit):
        return call(
            functools.partial(join_kernel, bit=bit), shape(heads * HD + LOGS, NS), 1, 2, 1
        )(place, first, second)

    near = far = jnp.zeros_like(packet)
    near_on = far_on = jnp.int32(0)
    total, group = packet, 1
    while group < n_seq:
        received = cross(total, group)
        on = (seq_pos // group) % 2
        if group * 2 == n_seq:
            far, far_on = received, on
        else:
            if n_seq == 4:
                near, near_on = received, on
            else:
                earlier = jnp.where(on == 1, received, jnp.zeros_like(received))
                near, near_on = earlier if group == 1 else join(near, earlier, 0), jnp.int32(1)
            total = join(total, received, group)
        group *= 2
    taken = jnp.stack([mp_pos, near_on, far_on]).astype(jnp.int32)

    query, gate_z = call(
        query_kernel,
        (shape(tokens, w_query.shape[1]), shape(tokens, inner_width)),
        0,
        5,
        2,
        left=1,
    )(normed, w_query, w_pair, cos, sin, b_mat)
    y_inside = call(inside_kernel, shape(tokens, inner_width, dtype=f32), 1, 5, 1)(
        d_skip, c_mat, b_mat, steps, cumulative, x_conv
    )

    if n_seq <= 4:
        attended = call(
            functools.partial(attention_kernel, cache_rows=cache_rows, scale=HD**-0.5),
            shape(tokens, w_query.shape[1]),
            2,
            1 + 2 * n_seq,
            6,
            scratch=[
                pltpu.VMEM((tokens * w_query.shape[1] // HD, n_seq * (cache_rows + tokens)), f32)
            ],
        )(place, cache_len, query, *mine, *other)
    else:
        is_key = mp_pos % 2 == 0
        attended = attend_plain(
            query,
            *[
                jnp.concatenate(
                    [both[:, :cache_rows].reshape(-1, HD), both[:, cache_rows:].reshape(-1, HD)], axis=0
                )
                for both in (
                    jnp.where(is_key, mine[0], other[0]),
                    jnp.where(is_key, other[0], mine[0]),
                )
            ],
            length,
            jnp.arange(n_seq),
            cache_rows,
            seq_pos,
        )

    state_after, mixed, far_x, far_y = call(
        finish_kernel,
        (
            shape(1, 1, heads, HD, NS, dtype=f32),
            shape(tokens, inner_width),
            shape(half, width),
            shape(half, width),
        ),
        1,
        12,
        3,
    )(
        taken, near, far, ssm_init, own_state, c_mat, cumulative, y_inside, gate_z, mixer_gain,
        attended, w_attn_out, w_mamba_out,
    )

    far_x_in = swap(far_x, 1)
    far_y_in = swap(far_y, 2)
    to_x, to_y = call(
        near_kernel, (shape(half, width), shape(half, width)), 1, 4, 1
    )(place, attended, mixed, w_attn_out, w_mamba_out)
    keep, keep_top, keep_low = call(
        keep_kernel,
        (
            shape(tokens, width, dtype=f32),
            shape(half, width, dtype=f32),
            shape(half, width, dtype=f32),
        ),
        1,
        5,
        1,
        left=1,
    )(place, attended, mixed, w_attn_out, w_mamba_out, own_rows, to_x)
    top_in = swap(to_x, 1)
    low_in = swap(to_y, 2)
    top_last = swap((keep_top + far_x_in.astype(f32)).astype(bf16), 2)
    low_last = swap((keep_low + far_y_in.astype(f32)).astype(bf16), 1)
    summed = keep + jnp.concatenate(
        [
            top_in.astype(f32) + top_last.astype(f32),
            low_in.astype(f32) + low_last.astype(f32),
        ],
        axis=0,
    )
    return (summed.astype(bf16)[None], kv_block[None], state_after)


def solution(mesh):
    placed = (
        P("req", "seq", "mp"),
        P(),
        P(None, "mp"),
        P(None, "mp"),
        P("mp", None),
        P(None, None, "mp"),
        P(None, "mp"),
        P(None, "mp"),
        P("mp"),
        P("mp"),
        P("mp"),
        P(None, "mp"),
        P(),
        P("mp"),
        P("mp", None),
        P("req", "seq", "mp"),
        P("req"),
        P("req", None, "mp"),
        P("req", None, None),
        P("req", "mp", None, None),
    )
    return jax.shard_map(
        shards,
        mesh=mesh,
        in_specs=placed,
        out_specs=(P("req", "seq", "mp"), P("req", "seq", "mp"), P("req", "seq", "mp", None, None)),
        check_vma=False,
    )
```

```python
import functools

import jax
import jax.numpy as jnp
from jax import lax
from jax.experimental import pallas as pl
from jax.experimental.pallas import tpu as pltpu
from jax.sharding import PartitionSpec as P

HD = 128
QH = 8
KVH = 2
NS = 256
CONV = 4
RIM = 16
LOGS = 32


epsilon = 1e-05
rope_base = 100000000000.0
negative = -1e30
f32 = jnp.float32
bf16 = jnp.bfloat16


def call(kernel, out_shape, n_scalars, n_arrays, micros, scratch=(), limit=24 * 1024 * 1024, left=0):
    smem = pl.BlockSpec(memory_space=pltpu.SMEM)
    vmem = pl.BlockSpec(memory_space=pltpu.VMEM)
    return pl.pallas_call(
        kernel,
        out_shape=out_shape,
        in_specs=[smem] * n_scalars + [vmem] * n_arrays + [pl.BlockSpec(memory_space=pl.ANY)] * left,
        out_specs=jax.tree.map(lambda _: vmem, out_shape),
        scratch_shapes=scratch,
        compiler_params=pltpu.CompilerParams(vmem_limit_bytes=limit),
        cost_estimate=pl.CostEstimate(flops=micros * 10**9, bytes_accessed=0, transcendentals=0),
    )


def shape(*dims, dtype=bf16):
    return jax.ShapeDtypeStruct(dims, dtype)


def swap(block, turn):
    return lax.ppermute(block, "mp", [(i, i ^ turn) for i in range(lax.axis_size("mp"))])


def cross(block, turn):
    return lax.ppermute(block, "seq", [(i, i ^ turn) for i in range(lax.axis_size("seq"))])


def ahead(block):
    count = lax.axis_size("seq")
    return lax.ppermute(block, "seq", [(i, (i + 1) % count) for i in range(count)])


def dot(a, b):
    return jnp.dot(a, b, preferred_element_type=f32)


def dot_nt(a, b):
    return lax.dot_general(a, b, (((1,), (1,)), ((), ())), preferred_element_type=f32)


def dot_tn(a, b):
    return lax.dot_general(a, b, (((0,), (0,)), ((), ())), preferred_element_type=f32)


def silu(v):
    return v / (1.0 + jnp.exp(-v))


def rope(v, cos, sin):
    return v * cos + pltpu.roll(v, HD // 2, 1) * sin


def pack_kernel(from_x, from_y, rim, *refs):
    to_y, to_x = refs[-2:]
    half = to_y.shape[0] - RIM
    to_y[:half, :] = from_x[:half]
    to_y[half:, :] = rim[...]
    to_x[:half, :] = from_y[half:]
    to_x[half:, :] = rim[...]


def norm_kernel(
    place, own, from_x, from_y, by_y, by_x, rim, diag_rim, gain, w_bc, w_kv, cos, sin,
    cache, later, normed, bc, kv, packed,
):
    me = place[0]
    tokens, width = own.shape
    half = tokens // 2
    full = 1.0 / (4 * width)

    def columns(turn):
        return pl.ds(pl.multiple_of((me ^ turn) * width, 128), width)

    def rows(start, count, blocks):
        size = min(count, 32)
        for at in range(0, count, size):
            parts = [block[at : at + size].astype(f32) for block in blocks]
            square = sum(
                part[:, lane : lane + 128] * part[:, lane : lane + 128]
                for part in parts
                for lane in range(0, width, 128)
            )
            inverse = lax.rsqrt(jnp.sum(square, axis=1, keepdims=True) * full + epsilon)
            for turn, part in enumerate(parts):
                scaled = part * inverse * gain[:, columns(turn)]
                normed[pl.ds(start + at, size), columns(turn)] = scaled.astype(bf16)

    rows(0, RIM, [rim[...], by_x[half:], by_y[half:], diag_rim[...]])
    rows(RIM, half, [own[:half], from_x[:half], from_y[:half], by_y[:half]])
    rows(RIM + half, half, [own[half:], from_x[half:], from_y[half:], by_x[:half]])
    both = None
    for at in range(0, 4 * width, width):
        weights = jnp.concatenate([w_bc[at : at + width], w_kv[at : at + width]], axis=1)
        part = dot(normed[:, at : at + width], weights)
        both = part if both is None else both + part
    bc[...] = both[:, :HD].astype(bf16)
    projected = both[RIM:, HD:]
    turned = rope(projected, cos[...], sin[...])
    block = jnp.where(me % 2 == 0, turned, projected).astype(bf16)
    kv[...] = block
    packed[: cache.shape[0], :] = cache[...]
    packed[cache.shape[0] :, :] = block


def softplus(v):
    return jnp.maximum(v, 0.0) + jnp.log1p(jnp.exp(-jnp.abs(v)))


def steps_kernel(dt_bias, a_log, normed, w_inner, w_dt, x_in, steps, cumulative):
    tokens = steps.shape[1]
    x_in[...] = dot(normed[...], w_inner[1]).astype(bf16)
    raw = jnp.concatenate([dot_nt(w_dt[...], normed[RIM:, :]), jnp.zeros((5, tokens), f32)], axis=0)
    head = lax.broadcasted_iota(jnp.int32, (8, tokens), 0)
    bias = jnp.zeros((8, tokens), f32)
    rate = jnp.zeros((8, tokens), f32)
    for h in range(3):
        bias = jnp.where(head == h, dt_bias[h], bias)
        rate = jnp.where(head == h, a_log[h], rate)
    step = softplus(raw + bias)
    decay = -step * jnp.exp(rate)
    before = lax.broadcasted_iota(jnp.int32, (tokens, tokens), 0)
    after = lax.broadcasted_iota(jnp.int32, (tokens, tokens), 1)
    upper = jnp.where(before <= after, 1.0, 0.0)
    steps[...] = step
    cumulative[...] = jnp.dot(
        decay, upper, preferred_element_type=f32, precision=lax.Precision.HIGHEST
    )


def query_kernel(normed, w_query, w_inner, cos, sin, *refs):
    query, gate_z = refs[-2:]
    current = normed[RIM:, :]
    gate_z[...] = dot(current, w_inner[0]).astype(bf16)
    projected = dot(current, w_query[...])
    for h in range(projected.shape[1] // HD):
        block = pl.ds(h * HD, HD)
        query[:, block] = rope(projected[:, h * HD : (h + 1) * HD], cos[...], sin[...]).astype(bf16)


def conv(scratch, tail, taps, first, tokens):
    scratch[RIM - CONV + 1 : RIM, :] = jnp.where(
        first, tail[0].astype(f32), scratch[RIM - CONV + 1 : RIM, :]
    )
    total = None
    for offset in range(CONV):
        start = RIM - CONV + 1 + offset
        term = taps[offset : offset + 1, :].astype(f32) * scratch[start : start + tokens, :]
        total = term if total is None else total + term
    return silu(total)


def logs_of(log):
    log = jnp.maximum(log, -256.0)
    high = jnp.floor(log)
    rest = (log - high) * 256.0
    middle = jnp.floor(rest)
    low = rest - middle
    return jnp.concatenate([high, middle, low, jnp.zeros_like(low)], axis=0).astype(bf16)


def log_from(rows):
    rows = rows.astype(f32)
    return rows[0:8] + (rows[8:16] + rows[16:24]) * (1.0 / 256.0)


def state_kernel(
    place, x_in, bc0, bc1, bc2, bc3, tail_x, tail_bc, conv_x, conv_bc, steps, cumulative,
    own, packet, x_conv, b_mat, c_mat, pad_x, pad_bc,
):
    me, first = place[0], place[1] == 0
    tokens = steps.shape[1]
    for turn, part in enumerate([bc0, bc1, bc2, bc3]):
        pad_bc[:, pl.ds(pl.multiple_of((me ^ turn) * HD, HD), HD)] = part[...].astype(f32)
    pad_x[...] = x_in[...].astype(f32)
    bc = conv(pad_bc, tail_bc, conv_bc, first, tokens).astype(bf16)
    b_mat[...] = bc[:, :NS]
    c_mat[...] = bc[:, NS:]
    convolved = conv(pad_x, tail_x, conv_x, first, tokens)
    x_conv[...] = convolved.astype(bf16)
    last = cumulative[:, tokens - 1 : tokens]
    to_end = jnp.transpose(jnp.exp(last - cumulative[...]) * steps[...])
    heads = convolved.shape[1] // HD
    for h in range(heads):
        weighted = convolved[:, h * HD : (h + 1) * HD] * to_end[:, h : h + 1]
        state = dot_tn(weighted.astype(bf16), bc[:, :NS])
        own[h * HD : (h + 1) * HD, :] = state
        packet[h * HD : (h + 1) * HD, :] = state.astype(bf16)
    packet[heads * HD :, :] = logs_of(jnp.broadcast_to(last, (8, NS)))


def inside_kernel(d_skip, c_mat, b_mat, steps, cumulative, x_conv, y):
    tokens = steps.shape[1]
    pairs = dot_nt(c_mat[...], b_mat[...])
    column = jnp.transpose(cumulative[...])
    row_id = lax.broadcasted_iota(jnp.int32, (tokens, tokens), 0)
    col_id = lax.broadcasted_iota(jnp.int32, (tokens, tokens), 1)
    lower = row_id >= col_id
    for h in range(x_conv.shape[1] // HD):
        gap = column[:, h : h + 1] - cumulative[h : h + 1, :]
        mixing = jnp.exp(jnp.where(lower, gap, negative)) * pairs * steps[h : h + 1, :]
        block = x_conv[:, h * HD : (h + 1) * HD]
        y[:, h * HD : (h + 1) * HD] = dot(mixing.astype(bf16), block) + d_skip[h] * block.astype(f32)


def join_kernel(place, first, second, packet, *, bit):
    swapped = (place[1] // bit) % 2 == 0 if bit else False
    size = first.shape[0] - LOGS
    first_log, second_log = log_from(first[size:, :]), log_from(second[size:, :])
    grown = jnp.exp(jnp.where(swapped, second_log, first_log))
    for h in range(size // HD):
        block = pl.ds(h * HD, HD)
        a, b = first[block, :].astype(f32), second[block, :].astype(f32)
        later, earlier = jnp.where(swapped, b, a), jnp.where(swapped, a, b)
        packet[block, :] = (later + grown[h : h + 1, :] * earlier).astype(bf16)
    packet[size:, :] = logs_of(first_log + second_log)


def term_of(me, attended, mixed, w_attn, w_mamba, width):
    def term(turn, start, count):
        columns = pl.ds(pl.multiple_of((me ^ turn) * width, 128), width)
        return dot(attended[start : start + count, :], w_attn[:, columns]) + dot(
            mixed[start : start + count, :], w_mamba[:, columns]
        )

    return term


def finish_kernel(
    place, near, far, init, c_mat, cumulative, y, gate_z, gain, attended, w_attn, w_mamba,
    incomes, mixed, far_x, far_y,
):
    me = place[0]
    heads = init.shape[1]
    tokens = y.shape[0]
    half = tokens // 2
    size = heads * HD
    near_on, far_on = place[1] == 1, place[2] == 1
    near_log = jnp.where(near_on, log_from(near[size:, :]), 0.0)
    far_log = jnp.where(far_on, log_from(far[size:, :]), 0.0)
    near_grown, far_grown = jnp.exp(near_log), jnp.exp(near_log + far_log)
    growth = jnp.transpose(jnp.exp(cumulative[...]))
    for h in range(heads):
        block = pl.ds(h * HD, HD)
        incoming = (
            jnp.where(near_on, near[block, :].astype(f32), 0.0)
            + near_grown[h : h + 1, :] * jnp.where(far_on, far[block, :].astype(f32), 0.0)
            + far_grown[h : h + 1, :] * init[0, h]
        )
        incomes[block, :] = incoming
        carried = dot_nt(c_mat[...], incoming.astype(bf16)) * growth[:, h : h + 1]
        gated = (y[:, block] + carried) * silu(gate_z[:, block].astype(f32))
        mean_sq = jnp.sum(gated * gated, axis=1, keepdims=True) * (1.0 / HD)
        mixed[:, block] = (gated * lax.rsqrt(mean_sq + epsilon) * gain[:, block]).astype(bf16)

    term = term_of(me, attended, mixed, w_attn, w_mamba, far_x.shape[1])
    far_x[...] = term(3, 0, half).astype(bf16)
    far_y[...] = term(3, half, half).astype(bf16)


def near_kernel(place, attended, mixed, w_attn, w_mamba, to_x, to_y):
    half, width = to_x.shape
    term = term_of(place[0], attended, mixed, w_attn, w_mamba, width)
    to_x[...] = term(1, 0, half).astype(bf16)
    to_y[...] = term(2, half, half).astype(bf16)


def keep_kernel(
    place, attended, mixed, w_attn, w_mamba, own, incomes, own_state, cumulative, sent,
    keep, keep_top, keep_low, states,
):
    last = cumulative.shape[1] - 1
    grown = jnp.exp(jnp.broadcast_to(cumulative[:, last : last + 1], (8, NS)))
    for h in range(states.shape[2]):
        block = pl.ds(h * HD, HD)
        states[0, 0, h] = grown[h : h + 1, :] * incomes[block, :] + own_state[block, :]
    tokens, width = own.shape
    half = tokens // 2
    term = term_of(place[0], attended, mixed, w_attn, w_mamba, width)
    keep_top[...] = term(2, 0, half)
    keep_low[...] = term(1, half, half)
    keep[...] = term(0, 0, tokens) + own[...].astype(f32)


def attention_kernel(place, length, query, *refs, cache_rows, scale):
    n_seq = (len(refs) - 2) // 2
    mine, other, out, scores = refs[:n_seq], refs[n_seq : 2 * n_seq], refs[-2], refs[-1]
    key_first = place[0] % 2 == 0
    seq_pos = place[1]
    tokens = query.shape[0]
    heads = query.shape[1] // HD
    rows = heads * tokens
    count = mine[0].shape[0]
    both = jnp.concatenate([query[:, h * HD : (h + 1) * HD] for h in range(heads)], axis=0)
    row = lax.broadcasted_iota(jnp.int32, (rows, count), 0) % tokens
    col = lax.broadcasted_iota(jnp.int32, (rows, count), 1)
    highest = None
    for turn in range(n_seq):
        keys = jnp.where(key_first, mine[turn][...], other[turn][...])
        owner = seq_pos ^ turn
        left = length[0] - owner * cache_rows
        last = cache_rows + jnp.where(owner < seq_pos, tokens, jnp.where(owner > seq_pos, -1, row))
        limit = jnp.where(col < cache_rows, left, last + 1)
        part = jnp.where(col < limit, dot_nt(both, keys), negative)
        scores[:, turn * count : (turn + 1) * count] = part
        for start in range(0, count, 128):
            block = part[:, start : start + 128]
            highest = block if highest is None else jnp.maximum(highest, block)
    top = jnp.max(highest, axis=1, keepdims=True)
    total = None
    accum = jnp.zeros((rows, HD), f32)
    for turn in range(n_seq):
        values = jnp.where(key_first, other[turn][...], mine[turn][...])
        weights = jnp.exp2((scores[:, turn * count : (turn + 1) * count] - top) * (scale * 1.4426950408889634))
        for start in range(0, count, 128):
            block = weights[:, start : start + 128]
            total = block if total is None else total + block
        accum = accum + dot(weights.astype(bf16), values)
    attended = accum / jnp.sum(total, axis=1, keepdims=True)
    for h in range(heads):
        out[:, h * HD : (h + 1) * HD] = attended[h * tokens : (h + 1) * tokens].astype(bf16)


def attend_plain(query, keys, values, length, starts, cache_rows, seq_pos):
    tokens = query.shape[0]
    query_index = seq_pos * tokens + jnp.arange(tokens, dtype=jnp.int32)
    slots = (starts[:, None] * cache_rows + jnp.arange(cache_rows, dtype=jnp.int32)).reshape(-1)
    news = (starts[:, None] * tokens + jnp.arange(tokens, dtype=jnp.int32)).reshape(-1)
    valid = jnp.concatenate(
        [
            jnp.broadcast_to((slots < length)[None], (tokens, slots.shape[0])),
            news[None, :] <= query_index[:, None],
        ],
        axis=1,
    )
    heads = query.reshape(tokens, -1, HD)
    scores = jnp.einsum("qhd,kd->hqk", heads, keys, preferred_element_type=f32) * HD**-0.5
    masked = jnp.where(valid[None], scores, negative)
    top = jnp.max(masked, axis=-1)
    weights = jnp.where(valid[None], jnp.exp(masked - top[:, :, None]), 0.0)
    total = jnp.sum(weights, axis=-1)
    accum = jnp.einsum("hqk,kd->hqd", weights.astype(bf16), values, preferred_element_type=f32)
    out = jnp.transpose(accum / total[:, :, None], (1, 0, 2)).reshape(tokens, -1)
    return out.astype(bf16)


def shards(
    hidden,
    norm_gain,
    w_query,
    w_keyval,
    w_attn_out,
    w_inner,
    w_bc,
    w_dt,
    dt_bias,
    a_log,
    d_skip,
    conv_x,
    conv_bc,
    mamba_gain,
    w_mamba_out,
    cache,
    cache_len,
    tail_x,
    tail_bc,
    ssm_init,
):
    own_rows = hidden[0]
    tokens, width = own_rows.shape
    half = tokens // 2
    seq_pos = lax.axis_index("seq")
    mp_pos = lax.axis_index("mp")
    n_seq = lax.axis_size("seq")
    length = cache_len[0]
    place = jnp.stack([mp_pos, seq_pos, jnp.int32(n_seq)]).astype(jnp.int32)
    inner_width = w_inner.shape[2]
    heads = inner_width // HD
    w_pair = jnp.transpose(w_inner, (1, 0, 2))

    from_x = swap(own_rows, 1)
    from_y = swap(own_rows, 2)
    rim = ahead(own_rows[tokens - RIM :])
    positions = length + seq_pos * tokens + jnp.arange(tokens, dtype=jnp.int32)
    freqs = rope_base ** (-jnp.arange(HD // 2, dtype=f32) * 2.0 / HD)
    angles = positions.astype(f32)[:, None] * jnp.concatenate([freqs, freqs])[None, :]
    cos = jnp.cos(angles)
    sin = jnp.where(jnp.arange(HD)[None, :] < HD // 2, -jnp.sin(angles), jnp.sin(angles))
    gain = norm_gain.astype(f32)[None, :]
    mixer_gain = mamba_gain.astype(f32)[None, :]

    to_y, to_x = call(
        pack_kernel, (shape(half + RIM, width), shape(half + RIM, width)), 0, 3, 3
    )(from_x, from_y, rim)
    by_y = swap(to_y, 2)
    by_x = swap(to_x, 1)
    diag_rim = swap(rim, 3)

    cache_rows = cache.shape[1]
    normed, bc_block, kv_block, packed = call(
        norm_kernel,
        (
            shape(RIM + tokens, 4 * width),
            shape(RIM + tokens, w_bc.shape[1]),
            shape(tokens, w_keyval.shape[1]),
            shape(cache_rows + tokens, w_keyval.shape[1]),
        ),
        1,
        13,
        3,
        left=1,
    )(
        place, own_rows, from_x, from_y, by_y, by_x, rim, diag_rim, gain, w_bc, w_keyval, cos, sin,
        cache[0], w_pair,
    )

    bc_parts = [bc_block] + [swap(bc_block, turn) for turn in (1, 2, 3)]

    x_in, steps, cumulative = call(
        steps_kernel,
        (
            shape(RIM + tokens, inner_width),
            shape(8, tokens, dtype=f32),
            shape(8, tokens, dtype=f32),
        ),
        2,
        3,
        2,
    )(dt_bias, a_log, normed, w_pair, w_dt.T)

    if n_seq <= 4:
        mine = [packed] + [cross(packed, turn) for turn in range(1, n_seq)]
    else:
        mine = [lax.all_gather(packed, "seq", axis=0)]
    other = [swap(block, 1) for block in mine]

    own_state, packet, x_conv, b_mat, c_mat = call(
        state_kernel,
        (
            shape(heads * HD, NS, dtype=f32),
            shape(heads * HD + LOGS, NS),
            shape(tokens, inner_width),
            shape(tokens, NS),
            shape(tokens, NS),
        ),
        1,
        11,
        2,
        scratch=[
            pltpu.VMEM((RIM + tokens, inner_width), f32),
            pltpu.VMEM((RIM + tokens, 2 * NS), f32),
        ],
    )(place, x_in, *bc_parts, tail_x, tail_bc, conv_x, conv_bc, steps, cumulative)

    def join(first, second, bit):
        return call(
            functools.partial(join_kernel, bit=bit), shape(heads * HD + LOGS, NS), 1, 2, 1
        )(place, first, second)

    near = far = jnp.zeros_like(packet)
    near_on = far_on = jnp.int32(0)
    total, group = packet, 1
    while group < n_seq:
        received = cross(total, group)
        on = (seq_pos // group) % 2
        if group * 2 == n_seq:
            far, far_on = received, on
        else:
            if n_seq == 4:
                near, near_on = received, on
            else:
                earlier = jnp.where(on == 1, received, jnp.zeros_like(received))
                near, near_on = earlier if group == 1 else join(near, earlier, 0), jnp.int32(1)
            total = join(total, received, group)
        group *= 2
    taken = jnp.stack([mp_pos, near_on, far_on]).astype(jnp.int32)

    query, gate_z = call(
        query_kernel,
        (shape(tokens, w_query.shape[1]), shape(tokens, inner_width)),
        0,
        5,
        2,
        left=1,
    )(normed, w_query, w_pair, cos, sin, b_mat)
    y_inside = call(inside_kernel, shape(tokens, inner_width, dtype=f32), 1, 5, 1)(
        d_skip, c_mat, b_mat, steps, cumulative, x_conv
    )

    if n_seq <= 4:
        attended = call(
            functools.partial(attention_kernel, cache_rows=cache_rows, scale=HD**-0.5),
            shape(tokens, w_query.shape[1]),
            2,
            1 + 2 * n_seq,
            6,
            scratch=[
                pltpu.VMEM((tokens * w_query.shape[1] // HD, n_seq * (cache_rows + tokens)), f32)
            ],
        )(place, cache_len, query, *mine, *other)
    else:
        is_key = mp_pos % 2 == 0
        attended = attend_plain(
            query,
            *[
                jnp.concatenate(
                    [both[:, :cache_rows].reshape(-1, HD), both[:, cache_rows:].reshape(-1, HD)], axis=0
                )
                for both in (
                    jnp.where(is_key, mine[0], other[0]),
                    jnp.where(is_key, other[0], mine[0]),
                )
            ],
            length,
            jnp.arange(n_seq),
            cache_rows,
            seq_pos,
        )

    incomes, mixed, far_x, far_y = call(
        finish_kernel,
        (
            shape(heads * HD, NS, dtype=f32),
            shape(tokens, inner_width),
            shape(half, width),
            shape(half, width),
        ),
        1,
        11,
        3,
    )(
        taken, near, far, ssm_init, c_mat, cumulative, y_inside, gate_z, mixer_gain,
        attended, w_attn_out, w_mamba_out,
    )

    far_x_in = swap(far_x, 1)
    far_y_in = swap(far_y, 2)
    to_x, to_y = call(
        near_kernel, (shape(half, width), shape(half, width)), 1, 4, 1
    )(place, attended, mixed, w_attn_out, w_mamba_out)
    keep, keep_top, keep_low, state_after = call(
        keep_kernel,
        (
            shape(tokens, width, dtype=f32),
            shape(half, width, dtype=f32),
            shape(half, width, dtype=f32),
            shape(1, 1, heads, HD, NS, dtype=f32),
        ),
        1,
        8,
        1,
        left=1,
    )(
        place, attended, mixed, w_attn_out, w_mamba_out, own_rows, incomes, own_state, cumulative, to_x
    )
    top_in = swap(to_x, 1)
    low_in = swap(to_y, 2)
    top_last = swap((keep_top + far_x_in.astype(f32)).astype(bf16), 2)
    low_last = swap((keep_low + far_y_in.astype(f32)).astype(bf16), 1)
    summed = keep + jnp.concatenate(
        [
            top_in.astype(f32) + top_last.astype(f32),
            low_in.astype(f32) + low_last.astype(f32),
        ],
        axis=0,
    )
    return (summed.astype(bf16)[None], kv_block[None], state_after)


def solution(mesh):
    placed = (
        P("req", "seq", "mp"),
        P(),
        P(None, "mp"),
        P(None, "mp"),
        P("mp", None),
        P(None, None, "mp"),
        P(None, "mp"),
        P(None, "mp"),
        P("mp"),
        P("mp"),
        P("mp"),
        P(None, "mp"),
        P(),
        P("mp"),
        P("mp", None),
        P("req", "seq", "mp"),
        P("req"),
        P("req", None, "mp"),
        P("req", None, None),
        P("req", "mp", None, None),
    )
    return jax.shard_map(
        shards,
        mesh=mesh,
        in_specs=placed,
        out_specs=(P("req", "seq", "mp"), P("req", "seq", "mp"), P("req", "seq", "mp", None, None)),
        check_vma=False,
    )
```

```python
import functools

import jax
import jax.numpy as jnp
from jax import lax
from jax.experimental import pallas as pl
from jax.experimental.pallas import tpu as pltpu
from jax.sharding import PartitionSpec as P

HD = 128
QH = 8
KVH = 2
NS = 256
CONV = 4
RIM = 16
LOGS = 32


epsilon = 1e-05
rope_base = 100000000000.0
negative = -1e30
f32 = jnp.float32
bf16 = jnp.bfloat16


def call(kernel, out_shape, n_scalars, n_arrays, micros, scratch=(), limit=24 * 1024 * 1024, left=0):
    smem = pl.BlockSpec(memory_space=pltpu.SMEM)
    vmem = pl.BlockSpec(memory_space=pltpu.VMEM)
    return pl.pallas_call(
        kernel,
        out_shape=out_shape,
        in_specs=[smem] * n_scalars + [vmem] * n_arrays + [pl.BlockSpec(memory_space=pl.ANY)] * left,
        out_specs=jax.tree.map(lambda _: vmem, out_shape),
        scratch_shapes=scratch,
        compiler_params=pltpu.CompilerParams(vmem_limit_bytes=limit),
        cost_estimate=pl.CostEstimate(flops=micros * 10**9, bytes_accessed=0, transcendentals=0),
    )


def shape(*dims, dtype=bf16):
    return jax.ShapeDtypeStruct(dims, dtype)


def swap(block, turn):
    return lax.ppermute(block, "mp", [(i, i ^ turn) for i in range(lax.axis_size("mp"))])


def cross(block, turn):
    return lax.ppermute(block, "seq", [(i, i ^ turn) for i in range(lax.axis_size("seq"))])


def ahead(block):
    count = lax.axis_size("seq")
    return lax.ppermute(block, "seq", [(i, (i + 1) % count) for i in range(count)])


def dot(a, b):
    return jnp.dot(a, b, preferred_element_type=f32)


def dot_nt(a, b):
    return lax.dot_general(a, b, (((1,), (1,)), ((), ())), preferred_element_type=f32)


def dot_tn(a, b):
    return lax.dot_general(a, b, (((0,), (0,)), ((), ())), preferred_element_type=f32)


def silu(v):
    return v / (1.0 + jnp.exp(-v))


def rope(v, cos, sin):
    return v * cos + pltpu.roll(v, HD // 2, 1) * sin


def pack_kernel(from_y, from_x, rim, *refs):
    to_y, to_x = refs[-2:]
    half = to_y.shape[0] - RIM
    to_y[:half, :] = from_x[:half]
    to_y[half:, :] = rim[...]
    to_x[:half, :] = from_y[half:]
    to_x[half:, :] = rim[...]


def norm_kernel(
    place, own, from_x, from_y, by_y, by_x, rim, diag_rim, gain, w_bc, w_kv, cos, sin,
    cache, later, normed, bc, kv, packed,
):
    me = place[0]
    tokens, width = own.shape
    half = tokens // 2
    full = 1.0 / (4 * width)

    def columns(turn):
        return pl.ds(pl.multiple_of((me ^ turn) * width, 128), width)

    def rows(start, count, blocks):
        size = min(count, 32)
        for at in range(0, count, size):
            parts = [block[at : at + size].astype(f32) for block in blocks]
            square = sum(
                part[:, lane : lane + 128] * part[:, lane : lane + 128]
                for part in parts
                for lane in range(0, width, 128)
            )
            inverse = lax.rsqrt(jnp.sum(square, axis=1, keepdims=True) * full + epsilon)
            for turn, part in enumerate(parts):
                scaled = part * inverse * gain[:, columns(turn)]
                normed[pl.ds(start + at, size), columns(turn)] = scaled.astype(bf16)

    rows(0, RIM, [rim[...], by_x[half:], by_y[half:], diag_rim[...]])
    rows(RIM, half, [own[:half], from_x[:half], from_y[:half], by_y[:half]])
    rows(RIM + half, half, [own[half:], from_x[half:], from_y[half:], by_x[:half]])
    both = None
    for at in range(0, 4 * width, width):
        weights = jnp.concatenate([w_bc[at : at + width], w_kv[at : at + width]], axis=1)
        part = dot(normed[:, at : at + width], weights)
        both = part if both is None else both + part
    bc[...] = both[:, :HD].astype(bf16)
    projected = both[RIM:, HD:]
    turned = rope(projected, cos[...], sin[...])
    block = jnp.where(me % 2 == 0, turned, projected).astype(bf16)
    kv[...] = block
    packed[: cache.shape[0], :] = cache[...]
    packed[cache.shape[0] :, :] = block


def softplus(v):
    return jnp.maximum(v, 0.0) + jnp.log1p(jnp.exp(-jnp.abs(v)))


def steps_kernel(dt_bias, a_log, normed, w_inner, w_dt, x_in, steps, cumulative):
    tokens = steps.shape[1]
    part = normed.shape[1] // 4
    x_in[...] = sum(
        dot(normed[:, at : at + part], w_inner[1, at : at + part]) for at in range(0, 4 * part, part)
    ).astype(bf16)
    raw = jnp.concatenate([dot_nt(w_dt[...], normed[RIM:, :]), jnp.zeros((5, tokens), f32)], axis=0)
    head = lax.broadcasted_iota(jnp.int32, (8, tokens), 0)
    bias = jnp.zeros((8, tokens), f32)
    rate = jnp.zeros((8, tokens), f32)
    for h in range(3):
        bias = jnp.where(head == h, dt_bias[h], bias)
        rate = jnp.where(head == h, a_log[h], rate)
    step = softplus(raw + bias)
    decay = -step * jnp.exp(rate)
    before = lax.broadcasted_iota(jnp.int32, (tokens, tokens), 0)
    after = lax.broadcasted_iota(jnp.int32, (tokens, tokens), 1)
    upper = jnp.where(before <= after, 1.0, 0.0)
    steps[...] = step
    cumulative[...] = jnp.dot(
        decay, upper, preferred_element_type=f32, precision=lax.Precision.HIGHEST
    )


def query_kernel(normed, w_query, w_inner, cos, sin, *refs):
    query, gate_z = refs[-2:]
    current = normed[RIM:, :]
    gate_z[...] = dot(current, w_inner[0]).astype(bf16)
    projected = dot(current, w_query[...])
    for h in range(projected.shape[1] // HD):
        block = pl.ds(h * HD, HD)
        query[:, block] = rope(projected[:, h * HD : (h + 1) * HD], cos[...], sin[...]).astype(bf16)


def conv(scratch, tail, taps, first, tokens):
    scratch[RIM - CONV + 1 : RIM, :] = jnp.where(
        first, tail[0].astype(f32), scratch[RIM - CONV + 1 : RIM, :]
    )
    total = None
    for offset in range(CONV):
        start = RIM - CONV + 1 + offset
        term = taps[offset : offset + 1, :].astype(f32) * scratch[start : start + tokens, :]
        total = term if total is None else total + term
    return silu(total)


def logs_of(log):
    log = jnp.maximum(log, -256.0)
    high = jnp.floor(log)
    rest = (log - high) * 256.0
    middle = jnp.floor(rest)
    low = rest - middle
    return jnp.concatenate([high, middle, low, jnp.zeros_like(low)], axis=0).astype(bf16)


def log_from(rows):
    rows = rows.astype(f32)
    return rows[0:8] + (rows[8:16] + rows[16:24]) * (1.0 / 256.0)


def state_kernel(
    place, x_in, bc0, bc1, bc2, bc3, tail_x, tail_bc, conv_x, conv_bc, steps, cumulative,
    own, packet, x_conv, b_mat, c_mat, pad_x, pad_bc,
):
    me, first = place[0], place[1] == 0
    tokens = steps.shape[1]
    for turn, part in enumerate([bc0, bc1, bc2, bc3]):
        pad_bc[:, pl.ds(pl.multiple_of((me ^ turn) * HD, HD), HD)] = part[...].astype(f32)
    pad_x[...] = x_in[...].astype(f32)
    bc = conv(pad_bc, tail_bc, conv_bc, first, tokens).astype(bf16)
    b_mat[...] = bc[:, :NS]
    c_mat[...] = bc[:, NS:]
    convolved = conv(pad_x, tail_x, conv_x, first, tokens)
    x_conv[...] = convolved.astype(bf16)
    last = cumulative[:, tokens - 1 : tokens]
    to_end = jnp.transpose(jnp.exp(last - cumulative[...]) * steps[...])
    heads = convolved.shape[1] // HD
    for h in range(heads):
        weighted = convolved[:, h * HD : (h + 1) * HD] * to_end[:, h : h + 1]
        state = dot_tn(weighted.astype(bf16), bc[:, :NS])
        own[h * HD : (h + 1) * HD, :] = state
        packet[h * HD : (h + 1) * HD, :] = state.astype(bf16)
    packet[heads * HD :, :] = logs_of(jnp.broadcast_to(last, (8, NS)))


def inside_kernel(d_skip, c_mat, b_mat, steps, cumulative, x_conv, y):
    tokens = steps.shape[1]
    pairs = dot_nt(c_mat[...], b_mat[...])
    column = jnp.transpose(cumulative[...])
    row_id = lax.broadcasted_iota(jnp.int32, (tokens, tokens), 0)
    col_id = lax.broadcasted_iota(jnp.int32, (tokens, tokens), 1)
    lower = row_id >= col_id
    for h in range(x_conv.shape[1] // HD):
        gap = column[:, h : h + 1] - cumulative[h : h + 1, :]
        mixing = jnp.exp(jnp.where(lower, gap, negative)) * pairs * steps[h : h + 1, :]
        block = x_conv[:, h * HD : (h + 1) * HD]
        y[:, h * HD : (h + 1) * HD] = dot(mixing.astype(bf16), block) + d_skip[h] * block.astype(f32)


def join_kernel(place, first, second, packet, *, bit):
    swapped = (place[1] // bit) % 2 == 0 if bit else False
    size = first.shape[0] - LOGS
    first_log, second_log = log_from(first[size:, :]), log_from(second[size:, :])
    grown = jnp.exp(jnp.where(swapped, second_log, first_log))
    for h in range(size // HD):
        block = pl.ds(h * HD, HD)
        a, b = first[block, :].astype(f32), second[block, :].astype(f32)
        later, earlier = jnp.where(swapped, b, a), jnp.where(swapped, a, b)
        packet[block, :] = (later + grown[h : h + 1, :] * earlier).astype(bf16)
    packet[size:, :] = logs_of(first_log + second_log)


def term_of(me, attended, mixed, w_attn, w_mamba, width):
    def term(turn, start, count):
        columns = pl.ds(pl.multiple_of((me ^ turn) * width, 128), width)
        return dot(attended[start : start + count, :], w_attn[:, columns]) + dot(
            mixed[start : start + count, :], w_mamba[:, columns]
        )

    return term


def finish_kernel(
    place, near, far, init, c_mat, cumulative, y, gate_z, gain, attended, w_attn, w_mamba,
    incomes, mixed, far_x, far_y,
):
    me = place[0]
    heads = init.shape[1]
    tokens = y.shape[0]
    half = tokens // 2
    size = heads * HD
    near_on, far_on = place[1] == 1, place[2] == 1
    near_log = jnp.where(near_on, log_from(near[size:, :]), 0.0)
    far_log = jnp.where(far_on, log_from(far[size:, :]), 0.0)
    near_grown, far_grown = jnp.exp(near_log), jnp.exp(near_log + far_log)
    growth = jnp.transpose(jnp.exp(cumulative[...]))
    for h in range(heads):
        block = pl.ds(h * HD, HD)
        incoming = (
            jnp.where(near_on, near[block, :].astype(f32), 0.0)
            + near_grown[h : h + 1, :] * jnp.where(far_on, far[block, :].astype(f32), 0.0)
            + far_grown[h : h + 1, :] * init[0, h]
        )
        incomes[block, :] = incoming
        carried = dot_nt(c_mat[...], incoming.astype(bf16)) * growth[:, h : h + 1]
        gated = (y[:, block] + carried) * silu(gate_z[:, block].astype(f32))
        mean_sq = jnp.sum(gated * gated, axis=1, keepdims=True) * (1.0 / HD)
        mixed[:, block] = (gated * lax.rsqrt(mean_sq + epsilon) * gain[:, block]).astype(bf16)

    term = term_of(me, attended, mixed, w_attn, w_mamba, far_x.shape[1])
    far_x[...] = term(3, 0, half).astype(bf16)
    far_y[...] = term(3, half, half).astype(bf16)


def near_kernel(place, attended, mixed, w_attn, w_mamba, to_x, to_y):
    half, width = to_x.shape
    term = term_of(place[0], attended, mixed, w_attn, w_mamba, width)
    to_x[...] = term(1, 0, half).astype(bf16)
    to_y[...] = term(2, half, half).astype(bf16)


def keep_kernel(
    place, attended, mixed, w_attn, w_mamba, own, incomes, own_state, cumulative, sent,
    keep, keep_top, keep_low, states,
):
    last = cumulative.shape[1] - 1
    grown = jnp.exp(jnp.broadcast_to(cumulative[:, last : last + 1], (8, NS)))
    for h in range(states.shape[2]):
        block = pl.ds(h * HD, HD)
        states[0, 0, h] = grown[h : h + 1, :] * incomes[block, :] + own_state[block, :]
    tokens, width = own.shape
    half = tokens // 2
    term = term_of(place[0], attended, mixed, w_attn, w_mamba, width)
    keep_top[...] = term(2, 0, half)
    keep_low[...] = term(1, half, half)
    keep[...] = term(0, 0, tokens) + own[...].astype(f32)


def attention_kernel(place, length, query, *refs, cache_rows, scale):
    n_seq = (len(refs) - 2) // 2
    mine, other, out, scores = refs[:n_seq], refs[n_seq : 2 * n_seq], refs[-2], refs[-1]
    key_first = place[0] % 2 == 0
    seq_pos = place[1]
    tokens = query.shape[0]
    heads = query.shape[1] // HD
    rows = heads * tokens
    count = mine[0].shape[0]
    both = jnp.concatenate([query[:, h * HD : (h + 1) * HD] for h in range(heads)], axis=0)
    row = lax.broadcasted_iota(jnp.int32, (rows, count), 0) % tokens
    col = lax.broadcasted_iota(jnp.int32, (rows, count), 1)
    highest = None
    for turn in range(n_seq):
        keys = jnp.where(key_first, mine[turn][...], other[turn][...])
        owner = seq_pos ^ turn
        left = length[0] - owner * cache_rows
        last = cache_rows + jnp.where(owner < seq_pos, tokens, jnp.where(owner > seq_pos, -1, row))
        limit = jnp.where(col < cache_rows, left, last + 1)
        part = jnp.where(col < limit, dot_nt(both, keys), negative)
        scores[:, turn * count : (turn + 1) * count] = part
        for start in range(0, count, 128):
            block = part[:, start : start + 128]
            highest = block if highest is None else jnp.maximum(highest, block)
    top = jnp.max(highest, axis=1, keepdims=True)
    total = None
    accum = jnp.zeros((rows, HD), f32)
    for turn in range(n_seq):
        values = jnp.where(key_first, other[turn][...], mine[turn][...])
        weights = jnp.exp2((scores[:, turn * count : (turn + 1) * count] - top) * (scale * 1.4426950408889634))
        for start in range(0, count, 128):
            block = weights[:, start : start + 128]
            total = block if total is None else total + block
        accum = accum + dot(weights.astype(bf16), values)
    attended = accum / jnp.sum(total, axis=1, keepdims=True)
    for h in range(heads):
        out[:, h * HD : (h + 1) * HD] = attended[h * tokens : (h + 1) * tokens].astype(bf16)


def attend_plain(query, keys, values, length, starts, cache_rows, seq_pos):
    tokens = query.shape[0]
    query_index = seq_pos * tokens + jnp.arange(tokens, dtype=jnp.int32)
    slots = (starts[:, None] * cache_rows + jnp.arange(cache_rows, dtype=jnp.int32)).reshape(-1)
    news = (starts[:, None] * tokens + jnp.arange(tokens, dtype=jnp.int32)).reshape(-1)
    valid = jnp.concatenate(
        [
            jnp.broadcast_to((slots < length)[None], (tokens, slots.shape[0])),
            news[None, :] <= query_index[:, None],
        ],
        axis=1,
    )
    heads = query.reshape(tokens, -1, HD)
    scores = jnp.einsum("qhd,kd->hqk", heads, keys, preferred_element_type=f32) * HD**-0.5
    masked = jnp.where(valid[None], scores, negative)
    top = jnp.max(masked, axis=-1)
    weights = jnp.where(valid[None], jnp.exp(masked - top[:, :, None]), 0.0)
    total = jnp.sum(weights, axis=-1)
    accum = jnp.einsum("hqk,kd->hqd", weights.astype(bf16), values, preferred_element_type=f32)
    out = jnp.transpose(accum / total[:, :, None], (1, 0, 2)).reshape(tokens, -1)
    return out.astype(bf16)


def shards(
    hidden,
    norm_gain,
    w_query,
    w_keyval,
    w_attn_out,
    w_inner,
    w_bc,
    w_dt,
    dt_bias,
    a_log,
    d_skip,
    conv_x,
    conv_bc,
    mamba_gain,
    w_mamba_out,
    cache,
    cache_len,
    tail_x,
    tail_bc,
    ssm_init,
):
    own_rows = hidden[0]
    tokens, width = own_rows.shape
    half = tokens // 2
    seq_pos = lax.axis_index("seq")
    mp_pos = lax.axis_index("mp")
    n_seq = lax.axis_size("seq")
    length = cache_len[0]
    place = jnp.stack([mp_pos, seq_pos, jnp.int32(n_seq)]).astype(jnp.int32)
    inner_width = w_inner.shape[2]
    heads = inner_width // HD
    w_pair = jnp.transpose(w_inner, (1, 0, 2))

    from_x = swap(own_rows, 1)
    from_y = swap(own_rows, 2)
    rim = ahead(own_rows[tokens - RIM :])
    positions = length + seq_pos * tokens + jnp.arange(tokens, dtype=jnp.int32)
    freqs = rope_base ** (-jnp.arange(HD // 2, dtype=f32) * 2.0 / HD)
    angles = positions.astype(f32)[:, None] * jnp.concatenate([freqs, freqs])[None, :]
    cos = jnp.cos(angles)
    sin = jnp.where(jnp.arange(HD)[None, :] < HD // 2, -jnp.sin(angles), jnp.sin(angles))
    gain = norm_gain.astype(f32)[None, :]
    mixer_gain = mamba_gain.astype(f32)[None, :]

    to_y, to_x = call(
        pack_kernel, (shape(half + RIM, width), shape(half + RIM, width)), 0, 3, 3
    )(from_y, from_x, rim)
    by_y = swap(to_y, 2)
    by_x = swap(to_x, 1)
    diag_rim = swap(rim, 3)

    cache_rows = cache.shape[1]
    normed, bc_block, kv_block, packed = call(
        norm_kernel,
        (
            shape(RIM + tokens, 4 * width),
            shape(RIM + tokens, w_bc.shape[1]),
            shape(tokens, w_keyval.shape[1]),
            shape(cache_rows + tokens, w_keyval.shape[1]),
        ),
        1,
        13,
        3,
        left=1,
    )(
        place, own_rows, from_x, from_y, by_y, by_x, rim, diag_rim, gain, w_bc, w_keyval, cos, sin,
        cache[0], w_pair,
    )

    bc_parts = [bc_block] + [swap(bc_block, turn) for turn in (1, 2, 3)]

    x_in, steps, cumulative = call(
        steps_kernel,
        (
            shape(RIM + tokens, inner_width),
            shape(8, tokens, dtype=f32),
            shape(8, tokens, dtype=f32),
        ),
        2,
        3,
        2,
    )(dt_bias, a_log, normed, w_pair, w_dt.T)

    if n_seq <= 4:
        mine = [packed] + [cross(packed, turn) for turn in range(1, n_seq)]
    else:
        mine = [lax.all_gather(packed, "seq", axis=0)]
    other = [swap(block, 1) for block in mine]

    own_state, packet, x_conv, b_mat, c_mat = call(
        state_kernel,
        (
            shape(heads * HD, NS, dtype=f32),
            shape(heads * HD + LOGS, NS),
            shape(tokens, inner_width),
            shape(tokens, NS),
            shape(tokens, NS),
        ),
        1,
        11,
        2,
        scratch=[
            pltpu.VMEM((RIM + tokens, inner_width), f32),
            pltpu.VMEM((RIM + tokens, 2 * NS), f32),
        ],
    )(place, x_in, *bc_parts, tail_x, tail_bc, conv_x, conv_bc, steps, cumulative)

    def join(first, second, bit):
        return call(
            functools.partial(join_kernel, bit=bit), shape(heads * HD + LOGS, NS), 1, 2, 1
        )(place, first, second)

    near = far = jnp.zeros_like(packet)
    near_on = far_on = jnp.int32(0)
    total, group = packet, 1
    while group < n_seq:
        received = cross(total, group)
        on = (seq_pos // group) % 2
        if group * 2 == n_seq:
            far, far_on = received, on
        else:
            if n_seq == 4:
                near, near_on = received, on
            else:
                earlier = jnp.where(on == 1, received, jnp.zeros_like(received))
                near, near_on = earlier if group == 1 else join(near, earlier, 0), jnp.int32(1)
            total = join(total, received, group)
        group *= 2
    taken = jnp.stack([mp_pos, near_on, far_on]).astype(jnp.int32)

    query, gate_z = call(
        query_kernel,
        (shape(tokens, w_query.shape[1]), shape(tokens, inner_width)),
        0,
        5,
        2,
        left=1,
    )(normed, w_query, w_pair, cos, sin, b_mat)
    y_inside = call(inside_kernel, shape(tokens, inner_width, dtype=f32), 1, 5, 1)(
        d_skip, c_mat, b_mat, steps, cumulative, x_conv
    )

    if n_seq <= 4:
        attended = call(
            functools.partial(attention_kernel, cache_rows=cache_rows, scale=HD**-0.5),
            shape(tokens, w_query.shape[1]),
            2,
            1 + 2 * n_seq,
            6,
            scratch=[
                pltpu.VMEM((tokens * w_query.shape[1] // HD, n_seq * (cache_rows + tokens)), f32)
            ],
        )(place, cache_len, query, *mine, *other)
    else:
        is_key = mp_pos % 2 == 0
        attended = attend_plain(
            query,
            *[
                jnp.concatenate(
                    [both[:, :cache_rows].reshape(-1, HD), both[:, cache_rows:].reshape(-1, HD)], axis=0
                )
                for both in (
                    jnp.where(is_key, mine[0], other[0]),
                    jnp.where(is_key, other[0], mine[0]),
                )
            ],
            length,
            jnp.arange(n_seq),
            cache_rows,
            seq_pos,
        )

    incomes, mixed, far_x, far_y = call(
        finish_kernel,
        (
            shape(heads * HD, NS, dtype=f32),
            shape(tokens, inner_width),
            shape(half, width),
            shape(half, width),
        ),
        1,
        11,
        3,
    )(
        taken, near, far, ssm_init, c_mat, cumulative, y_inside, gate_z, mixer_gain,
        attended, w_attn_out, w_mamba_out,
    )

    far_x_in = swap(far_x, 1)
    far_y_in = swap(far_y, 2)
    to_x, to_y = call(
        near_kernel, (shape(half, width), shape(half, width)), 1, 4, 1
    )(place, attended, mixed, w_attn_out, w_mamba_out)
    keep, keep_top, keep_low, state_after = call(
        keep_kernel,
        (
            shape(tokens, width, dtype=f32),
            shape(half, width, dtype=f32),
            shape(half, width, dtype=f32),
            shape(1, 1, heads, HD, NS, dtype=f32),
        ),
        1,
        8,
        1,
        left=1,
    )(
        place, attended, mixed, w_attn_out, w_mamba_out, own_rows, incomes, own_state, cumulative, to_x
    )
    top_in = swap(to_x, 1)
    low_in = swap(to_y, 2)
    top_last = swap((keep_top + far_x_in.astype(f32)).astype(bf16), 2)
    low_last = swap((keep_low + far_y_in.astype(f32)).astype(bf16), 1)
    summed = keep + jnp.concatenate(
        [
            top_in.astype(f32) + top_last.astype(f32),
            low_in.astype(f32) + low_last.astype(f32),
        ],
        axis=0,
    )
    return (summed.astype(bf16)[None], kv_block[None], state_after)


def solution(mesh):
    placed = (
        P("req", "seq", "mp"),
        P(),
        P(None, "mp"),
        P(None, "mp"),
        P("mp", None),
        P(None, None, "mp"),
        P(None, "mp"),
        P(None, "mp"),
        P("mp"),
        P("mp"),
        P("mp"),
        P(None, "mp"),
        P(),
        P("mp"),
        P("mp", None),
        P("req", "seq", "mp"),
        P("req"),
        P("req", None, "mp"),
        P("req", None, None),
        P("req", "mp", None, None),
    )
    return jax.shard_map(
        shards,
        mesh=mesh,
        in_specs=placed,
        out_specs=(P("req", "seq", "mp"), P("req", "seq", "mp"), P("req", "seq", "mp", None, None)),
        check_vma=False,
    )
```
